32 devices in a mesh: groups: 2 (over y), seq: 8 (over z, x), cache: 2 (over core).
Axes of the slice: x: 2, y: 2, z: 4, core: 2. Of those that a mesh axis runs over, the one named last changes fastest.
Arguments:
- queries: bfloat16 [128, 2048, 128], P('groups', ('seq', 'cache')), parts along dimension 0, may hold values from -8 to 8
- stretch_keys: bfloat16 [128, 2048, 128], P('groups', 'seq'), parts along dimension 0, may hold values from -8 to 8
- stretch_values: bfloat16 [128, 2048, 128], P('groups', 'seq'), parts along dimension 0, may hold values from -6 to 6
- cache_keys: bfloat16 [128, 2048, 128], P(('groups', 'seq'), 'cache'), parts along dimension 0, may hold values from -6 to 6
- cache_values: bfloat16 [128, 2048, 128], P(('groups', 'seq'), 'cache'), parts along dimension 0, may hold values from -6 to 6
- rand_blocks: int32 [32, 3], P('groups'), parts along dimension 0, may hold values from 2 to 28, as said below
Outputs:
- attended: bfloat16 [128, 2048, 128], P('groups', ('seq', 'cache')), parts along dimension 0
The draws below stay inside these ranges and needn't reach their ends.
There are 2 independent parts, one for each index of `groups`. The reference program is written for one: setup_inputs(seed, part) draws one part's arguments, and reference() takes and returns one part's arrays. A program takes and returns all parts, laid end to end along the dimension named above; each array names one. Nothing has to cross between parts.
Inputs may be any that keep to these rules, and one draw needn't show every extreme that they name: `rand_blocks`: row i holds 3 different block numbers, each at least 2 and below 16 + i - 2.
All inputs are finite; a program needn't handle non-finite values.
Results may differ from the reference program's by a relative error of at most 0.0049.
Values may be sent and summed in bfloat16 or wider, within the bound.
No kernel may reach another device: no remote copies, remote signals or barrier semaphores. Data moves between devices by JAX's collectives and lax.ppermute only.
A program may use at most 128 MiB of HBM per device.

```python
import math
import jax
import jax.numpy as jnp
from jax import lax

DH = 128
BLK = 128
NR = 3
CB = 16
L = 2048
QB = 16
CLEN = 2048
PAIRS = 64


def draw_queries(key, part):
    sample = jnp.clip(jax.random.normal(jax.random.fold_in(key, 1), (PAIRS, L, DH), jnp.float32), -4.5, 4.5)
    return sample.astype(jnp.bfloat16)


def draw_stretch_keys(key, part):
    sample = jnp.clip(jax.random.normal(jax.random.fold_in(key, 2), (PAIRS, L, DH), jnp.float32), -4.5, 4.5)
    return sample.astype(jnp.bfloat16)


def draw_rand_blocks(key, part):
    block_index = jnp.arange(QB, dtype=jnp.int32)[:, None]
    column = jnp.arange(NR, dtype=jnp.int32)[None, :]
    span = CB + block_index - 4
    stratum = span // NR
    drawn = jax.random.randint(key, (QB, NR), 0, 1 << 20, dtype=jnp.int32) % stratum
    drawn = jnp.where((block_index == 0) & (column == 0), 0, drawn)
    drawn = jnp.where((block_index == QB - 1) & (column == NR - 1), stratum - 1, drawn)
    return 2 + column * stratum + drawn


def steps_of(rng, dims, split, low, largest):
    factor_of, own = 1.0, jax.random.fold_in(rng, 6)
    for dim, shards_of in split:
        draws = jnp.exp(jax.random.uniform(jax.random.fold_in(own, dim), (shards_of,), jnp.float32, low / len(split), largest / len(split)))
        factor_of = factor_of * jnp.repeat(draws, dims[dim] // shards_of).reshape([-1 if axis == dim else 1 for axis in range(len(dims))])
    return factor_of


def normal_values(rng, shape, spread, reach, pieces=(), kind=jnp.bfloat16):
    level = steps_of(rng, shape, pieces, -0.22, 0.18) if pieces else 1.0
    entries = jax.random.normal(rng, shape, jnp.float32) * spread * level
    return jnp.minimum(jnp.maximum(entries, -reach), reach).astype(kind)


def setup_inputs(seed: int = 0, part: int = 0) -> dict:
    keys = jax.random.split(jax.random.key(seed), 7)
    own_keys = jax.random.split(jax.random.fold_in(keys[6], part), 7)
    queries = draw_queries(jax.random.fold_in(jax.random.fold_in(keys[6], part), 71), part)
    stretch_keys = draw_stretch_keys(jax.random.fold_in(jax.random.fold_in(keys[6], part), 71), part)
    stretch_values = normal_values(own_keys[2], (PAIRS, L, DH), 1.0, 6.0, ((1, 8),))
    cache_keys = normal_values(own_keys[3], (PAIRS, CLEN, DH), 1.0, 6.0, ((0, 8), (1, 2)))
    cache_values = normal_values(own_keys[4], (PAIRS, CLEN, DH), 1.0, 6.0, ((0, 8), (1, 2)))
    rand_blocks = draw_rand_blocks(jax.random.fold_in(jax.random.fold_in(keys[6], part), 71), part)
    return dict(queries=queries, stretch_keys=stretch_keys, stretch_values=stretch_values, cache_keys=cache_keys, cache_values=cache_values, rand_blocks=rand_blocks)


def block_lists(rand_blocks):
    block_count = rand_blocks.shape[0]
    starts = jnp.arange(block_count, dtype=jnp.int32)[:, None] + CB
    window = starts + jnp.array([-2, -1, 0], jnp.int32)[None, :]
    anchors = jnp.broadcast_to(jnp.array([0, 1], jnp.int32)[None, :], (block_count, 2))
    return jnp.concatenate([window, anchors, rand_blocks.astype(jnp.int32)], axis=1)

def attend_blocks(query_blocks, key_lists, key_blocks, value_blocks):
    groups, block_width, head_width = query_blocks.shape
    listed = key_lists.shape[1]
    chosen_keys = jnp.take(key_blocks, key_lists, axis=0).reshape(groups, listed * block_width, head_width)
    chosen_values = jnp.take(value_blocks, key_lists, axis=0).reshape(groups, listed * block_width, head_width)
    scores = jnp.einsum('gqd,gkd->gqk', query_blocks.astype(jnp.float32), chosen_keys.astype(jnp.float32))
    scores = scores * (1.0 / math.sqrt(head_width))
    key_slot = jnp.arange(listed * block_width, dtype=jnp.int32)
    query_slot = jnp.arange(block_width, dtype=jnp.int32)
    blocked = (key_slot // block_width == 2)[None, :] & ((key_slot % block_width)[None, :] > query_slot[:, None])
    scores = jnp.where(blocked[None], -jnp.inf, scores)
    row_max = lax.optimization_barrier(jnp.max(scores, axis=2, keepdims=True))
    weights = jnp.exp(scores - row_max)
    row_probs = (weights / lax.optimization_barrier(jnp.sum(weights, axis=2, keepdims=True))).astype(jnp.bfloat16)
    result = jnp.einsum('gqk,gkd->gqd', row_probs.astype(jnp.float32), chosen_values.astype(jnp.float32))
    return result.astype(jnp.bfloat16)

def reference(queries, stretch_keys, stretch_values, cache_keys, cache_values, rand_blocks):
    key_lists = block_lists(rand_blocks)

    def one_pair(operands):
        query_rows, key_rows, value_rows, prefix_key, prefix_value = operands
        key_blocks = jnp.concatenate([prefix_key, key_rows], axis=0).reshape(-1, BLK, DH)
        value_blocks = jnp.concatenate([prefix_value, value_rows], axis=0).reshape(-1, BLK, DH)
        result = attend_blocks(query_rows.reshape(QB, BLK, DH), key_lists, key_blocks, value_blocks)
        return result.reshape(L, DH)
    return lax.map(one_pair, (queries, stretch_keys, stretch_values, cache_keys, cache_values))
```

```python
import math
import functools

import jax
import jax.numpy as jnp
from jax import lax
from jax.experimental import pallas as pl
from jax.experimental.pallas import tpu as pltpu
from jax.sharding import PartitionSpec as P

BLK = 128
LISTED = 8


def attention_kernel(place, rand, mine, theirs, ck_mine, ck_theirs, cv_mine, cv_theirs, out, keys, values):
    sources = mine.shape[0]
    cached = ck_mine.shape[1] // BLK
    prefix = 2 * cached
    side = place[0]
    other = 1 - side
    for index in range(cached):
        rows = pl.ds(index * BLK, BLK)
        keys[side * cached + index] = ck_mine[0, rows, :]
        values[side * cached + index] = cv_mine[0, rows, :]
        keys[other * cached + index] = ck_theirs[0, rows, :]
        values[other * cached + index] = cv_theirs[0, rows, :]

    def place_source(source, carry):
        block = prefix + 2 * source
        keys[block + side] = mine[source, 1, 0]
        values[block + side] = mine[source, 2, 0]
        keys[block + other] = theirs[source, 0, 0]
        values[block + other] = theirs[source, 1, 0]
        return carry

    lax.fori_loop(0, sources, place_source, 0, unroll=min(8, sources))
    scale = 1.0 / math.sqrt(mine.shape[-1])
    query_slot = lax.broadcasted_iota(jnp.int32, (BLK, BLK), 0)
    key_slot = lax.broadcasted_iota(jnp.int32, (BLK, BLK), 1)
    blocked = key_slot > query_slot

    def one_block(source, carry):
        block = 2 * source + side
        own = prefix + block
        listed = [own - 2, own - 1, own, 0, 1] + [rand[block, column] for column in range(3)]
        query = mine[source, 0, 0]
        parts = []
        for slot, key_block in enumerate(listed):
            part = lax.dot_general(
                query, keys[key_block], (((1,), (1,)), ((), ())), preferred_element_type=jnp.float32
            )
            part = part * scale
            if slot == 2:
                part = jnp.where(blocked, -jnp.inf, part)
            parts.append(part)
        scores = jnp.concatenate(parts, axis=1)
        row_max = jnp.max(scores, axis=1, keepdims=True)
        weights = jnp.exp(scores - row_max)
        inverse = 1.0 / jnp.sum(weights, axis=1, keepdims=True)
        probs = (weights * inverse).astype(jnp.bfloat16)
        total = jnp.zeros((BLK, mine.shape[-1]), jnp.float32)
        for slot, key_block in enumerate(listed):
            total += jnp.dot(
                probs[:, slot * BLK : (slot + 1) * BLK],
                values[key_block],
                preferred_element_type=jnp.float32,
            )
        out[source, 0] = total.astype(out.dtype)
        return carry

    lax.fori_loop(0, sources, one_block, 0, unroll=2)


def attend(place, rand, mine, theirs, caches, first):
    sources, _, heads, _, width = mine.shape
    cached_rows = caches[0].shape[1]
    key_blocks = 2 * cached_rows // BLK + 2 * sources
    cache_spec = pl.BlockSpec((1, cached_rows, width), lambda head, *_: (first + head, 0, 0))
    work = heads * sources * BLK * LISTED * BLK
    return pl.pallas_call(
        attention_kernel,
        grid_spec=pltpu.PrefetchScalarGridSpec(
            num_scalar_prefetch=2,
            grid=(heads,),
            in_specs=[
                pl.BlockSpec((sources, 3, 1, BLK, width), lambda head, *_: (0, 0, head, 0, 0)),
                pl.BlockSpec((sources, 2, 1, BLK, width), lambda head, *_: (0, 0, head, 0, 0)),
            ]
            + [cache_spec] * 4,
            out_specs=pl.BlockSpec((sources, 1, BLK, width), lambda head, *_: (0, head, 0, 0)),
            scratch_shapes=[
                pltpu.VMEM((key_blocks, BLK, width), jnp.bfloat16),
                pltpu.VMEM((key_blocks, BLK, width), jnp.bfloat16),
            ],
        ),
        out_shape=jax.ShapeDtypeStruct((sources, heads, BLK, width), jnp.bfloat16),
        compiler_params=pltpu.CompilerParams(vmem_limit_bytes=48 * 1024 * 1024),
        cost_estimate=pl.CostEstimate(
            flops=4 * work * width,
            bytes_accessed=2 * heads * width * BLK * (6 * sources + 2 * key_blocks),
            transcendentals=work,
        ),
    )(place, rand, mine, theirs, *caches)


def per_device(queries, stretch_keys, stretch_values, cache_keys, cache_values, rand_blocks):
    heads, local_rows, width = queries.shape
    seq_devices = lax.axis_size("seq")
    side = lax.axis_index("cache")
    owned = heads // seq_devices
    swap = [(0, 1), (1, 0)]
    assert local_rows == BLK and lax.axis_size("cache") == 2

    def own_rows(rows):
        return lax.dynamic_slice_in_dim(rows, side * local_rows, local_rows, axis=1)

    def by_owner(rows):
        return rows.reshape(seq_devices, owned, local_rows, width)

    packed = jnp.stack(
        [by_owner(queries), by_owner(own_rows(stretch_keys)), by_owner(own_rows(stretch_values))], axis=1
    )
    caches = (
        cache_keys,
        lax.ppermute(cache_keys, "cache", swap),
        cache_values,
        lax.ppermute(cache_values, "cache", swap),
    )
    place = jnp.reshape(side, (1,)).astype(jnp.int32)
    chunk = max(1, owned // 2)
    results = []
    for first in range(0, owned, chunk):
        mine = lax.all_to_all(
            packed[:, :, first : first + chunk], "seq", split_axis=0, concat_axis=0, tiled=True
        )
        theirs = lax.ppermute(mine[:, 1:], "cache", swap)
        attended = attend(place, rand_blocks, mine, theirs, caches, first)
        results.append(lax.all_to_all(attended, "seq", split_axis=0, concat_axis=0, tiled=True))
    return jnp.concatenate(results, axis=1).reshape(heads, local_rows, width)


def solution(mesh):
    placed = (
        P("groups", ("seq", "cache"), None),
        P("groups", "seq", None),
        P("groups", "seq", None),
        P(("groups", "seq"), "cache", None),
        P(("groups", "seq"), "cache", None),
        P("groups", None),
    )
    return jax.shard_map(
        per_device,
        mesh=mesh,
        in_specs=placed,
        out_specs=P("groups", ("seq", "cache"), None),
        check_vma=False,
    )
```

```python
import math

import jax
import jax.numpy as jnp
from jax import lax
from jax.experimental import pallas as pl
from jax.experimental.pallas import tpu as pltpu
from jax.sharding import PartitionSpec as P

BLK = 128
LISTED = 8
CHUNKS = 2
WINDOW = 4


def attention_kernel(pieces, place, rand, *refs):
    mine, refs = refs[:pieces], refs[pieces:]
    theirs, refs = refs[:pieces], refs[pieces:]
    (ck_mine, ck_theirs, cv_mine, cv_theirs), refs = refs[:4], refs[4:]
    outs, (queries, results, keys, values) = refs[:pieces], refs[pieces:]
    per_piece = mine[0].shape[0]
    sources = pieces * per_piece
    cached = ck_mine.shape[1] // BLK
    prefix = 2 * cached
    side = place[sources]
    other = 1 - side
    for index in range(cached):
        rows = pl.ds(index * BLK, BLK)
        keys[side * cached + index] = ck_mine[0, rows, :]
        values[side * cached + index] = cv_mine[0, rows, :]
        keys[other * cached + index] = ck_theirs[0, rows, :]
        values[other * cached + index] = cv_theirs[0, rows, :]

    for piece in range(pieces):
        for index in range(per_piece):
            slot = piece * per_piece + index
            block = prefix + 2 * place[slot]
            queries[slot] = mine[piece][index, 0, 0]
            keys[block + side] = mine[piece][index, 1, 0]
            values[block + side] = mine[piece][index, 2, 0]
            keys[block + other] = theirs[piece][index, 1, 0]
            values[block + other] = theirs[piece][index, 2, 0]

    width = queries.shape[-1]
    scale = 1.0 / math.sqrt(width)
    query_slot = lax.broadcasted_iota(jnp.int32, (BLK, BLK), 0)
    key_slot = lax.broadcasted_iota(jnp.int32, (BLK, BLK), 1)
    blocked = key_slot > query_slot

    def one_block(slot, carry):
        block = 2 * place[slot] + side
        own = prefix + block
        listed = [own - 2, own - 1, own, 0, 1] + [rand[block, column] for column in range(3)]
        query = queries[slot]
        parts = []
        for position, key_block in enumerate(listed):
            part = lax.dot_general(
                query, keys[key_block], (((1,), (1,)), ((), ())), preferred_element_type=jnp.float32
            )
            part = part * scale
            if position == 2:
                part = jnp.where(blocked, -jnp.inf, part)
            parts.append(part)
        scores = jnp.concatenate(parts, axis=1)
        row_max = jnp.max(scores, axis=1, keepdims=True)
        weights = jnp.exp(scores - row_max)
        inverse = 1.0 / jnp.sum(weights, axis=1, keepdims=True)
        probs = (weights * inverse).astype(jnp.bfloat16)
        total = jnp.zeros((BLK, width), jnp.float32)
        for position, key_block in enumerate(listed):
            total += jnp.dot(
                probs[:, position * BLK : (position + 1) * BLK],
                values[key_block],
                preferred_element_type=jnp.float32,
            )
        results[slot] = total.astype(jnp.bfloat16)
        return carry

    lax.fori_loop(0, sources, one_block, 0, unroll=2)
    for piece in range(pieces):
        for index in range(per_piece):
            outs[piece][index, 0] = results[piece * per_piece + index]


def attend(place, rand, mine, theirs, caches, first):
    pieces = len(mine)
    per_piece, parts, heads, _, width = mine[0].shape
    sources = pieces * per_piece
    cached_rows = caches[0].shape[1]
    key_blocks = 2 * cached_rows // BLK + 2 * sources
    cache_spec = pl.BlockSpec((1, cached_rows, width), lambda head, *_: (first + head, 0, 0))
    piece_spec = pl.BlockSpec((per_piece, parts, 1, BLK, width), lambda head, *_: (0, 0, head, 0, 0))
    out_spec = pl.BlockSpec((per_piece, 1, BLK, width), lambda head, *_: (0, head, 0, 0))
    work = heads * sources * BLK * LISTED * BLK

    def kernel(*refs):
        attention_kernel(pieces, *refs)

    return pl.pallas_call(
        kernel,
        grid_spec=pltpu.PrefetchScalarGridSpec(
            num_scalar_prefetch=2,
            grid=(heads,),
            in_specs=[piece_spec] * (2 * pieces) + [cache_spec] * 4,
            out_specs=[out_spec] * pieces,
            scratch_shapes=[
                pltpu.VMEM((sources, BLK, width), jnp.bfloat16),
                pltpu.VMEM((sources, BLK, width), jnp.bfloat16),
                pltpu.VMEM((key_blocks, BLK, width), jnp.bfloat16),
                pltpu.VMEM((key_blocks, BLK, width), jnp.bfloat16),
            ],
        ),
        out_shape=[jax.ShapeDtypeStruct((per_piece, heads, BLK, width), jnp.bfloat16)] * pieces,
        compiler_params=pltpu.CompilerParams(vmem_limit_bytes=48 * 1024 * 1024),
        cost_estimate=pl.CostEstimate(
            flops=4 * work * width,
            bytes_accessed=2 * heads * width * BLK * (6 * sources + 2 * key_blocks),
            transcendentals=work,
        ),
    )(place, rand, *mine, *theirs, *caches)


def after(value, *earlier):
    return lax.optimization_barrier((value, *earlier))[0]


def per_device(queries, stretch_keys, stretch_values, cache_keys, cache_values, rand_blocks):
    heads, local_rows, width = queries.shape
    seq_devices = lax.axis_size("seq")
    here = lax.axis_index("seq")
    side = lax.axis_index("cache")
    owned = heads // seq_devices
    swap = [(0, 1), (1, 0)]
    assert local_rows == BLK and lax.axis_size("cache") == 2

    def own_rows(rows):
        return lax.dynamic_slice_in_dim(rows, side * local_rows, local_rows, axis=1)

    def by_owner(rows):
        return rows.reshape(seq_devices, owned, local_rows, width)

    caches = (
        cache_keys,
        lax.ppermute(cache_keys, "cache", swap),
        cache_values,
        lax.ppermute(cache_values, "cache", swap),
    )

    if seq_devices > 8 or seq_devices & (seq_devices - 1) or owned % CHUNKS:
        packed = jnp.stack(
            [by_owner(queries), by_owner(own_rows(stretch_keys)), by_owner(own_rows(stretch_values))], axis=1
        )
        place = jnp.concatenate([jnp.arange(seq_devices, dtype=jnp.int32), jnp.reshape(side, (1,)).astype(jnp.int32)])
        mine = lax.all_to_all(packed, "seq", split_axis=0, concat_axis=0, tiled=True)
        theirs = lax.ppermute(mine, "cache", swap)
        attended = attend(place, rand_blocks, [mine], [theirs], caches, 0)[0]
        returned = lax.all_to_all(attended, "seq", split_axis=0, concat_axis=0, tiled=True)
        return returned.reshape(heads, local_rows, width)

    partners = [here ^ step for step in range(seq_devices)]
    place = jnp.stack(partners + [side]).astype(jnp.int32)
    order = [4, 1, 5, 2, 6, 3, 7] if seq_devices == 8 else list(range(1, seq_devices))
    chunk = owned // CHUNKS

    def to_partner(value, step):
        return lax.ppermute(value, "seq", [(index, index ^ step) for index in range(seq_devices)])

    def packed(step, first):
        start = partners[step] * owned + first
        return jnp.stack(
            [
                lax.dynamic_slice(queries, (start, 0, 0), (chunk, local_rows, width)),
                lax.dynamic_slice(stretch_keys, (start, side * local_rows, 0), (chunk, local_rows, width)),
                lax.dynamic_slice(stretch_values, (start, side * local_rows, 0), (chunk, local_rows, width)),
            ]
        )[None]

    sent = []
    result = jnp.zeros((heads, local_rows, width), jnp.bfloat16)
    for first in range(0, owned, chunk):
        mine = [packed(0, first)] + [None] * (seq_devices - 1)
        for step in order:
            message = packed(step, first)
            if len(sent) >= WINDOW:
                message = after(message, sent[-WINDOW])
            mine[step] = to_partner(message, step)
            sent.append(mine[step])
        theirs = [lax.ppermute(piece, "cache", swap) for piece in mine]
        attended = attend(place, rand_blocks, mine, theirs, caches, first)
        for step in [0] + order:
            returned = attended[step][0] if step == 0 else to_partner(attended[step], step)[0]
            result = lax.dynamic_update_slice(result, returned, (partners[step] * owned + first, 0, 0))
    return result


def solution(mesh):
    placed = (
        P("groups", ("seq", "cache"), None),
        P("groups", "seq", None),
        P("groups", "seq", None),
        P(("groups", "seq"), "cache", None),
        P(("groups", "seq"), "cache", None),
        P("groups", None),
    )
    return jax.shard_map(
        per_device,
        mesh=mesh,
        in_specs=placed,
        out_specs=P("groups", ("seq", "cache"), None),
        check_vma=False,
    )
```

```python
import math

import jax
import jax.numpy as jnp
from jax import lax
from jax.experimental import pallas as pl
from jax.experimental.pallas import tpu as pltpu
from jax.sharding import PartitionSpec as P

BLK = 128
LISTED = 8
PACK_VMEM = 60 * 1024 * 1024


def attention_kernel(
    place, rand, queries, keys_mine, values_mine, keys_theirs, values_theirs, ck_mine, ck_theirs, cv_mine, cv_theirs, out, keys, values
):
    sources = queries.shape[0]
    cached = ck_mine.shape[1] // BLK
    prefix = 2 * cached
    side = place[0]
    other = 1 - side
    for index in range(cached):
        rows = pl.ds(index * BLK, BLK)
        keys[side * cached + index] = ck_mine[0, rows, :]
        values[side * cached + index] = cv_mine[0, rows, :].T
        keys[other * cached + index] = ck_theirs[0, rows, :]
        values[other * cached + index] = cv_theirs[0, rows, :].T

    def place_source(source, carry):
        block = prefix + 2 * source
        keys[block + side] = keys_mine[source, 0, 0]
        values[block + side] = values_mine[source, 0, 0].T
        keys[block + other] = keys_theirs[source, 0, 0]
        values[block + other] = values_theirs[source, 0, 0].T
        return carry

    lax.fori_loop(0, sources, place_source, 0, unroll=min(8, sources))
    factor = math.log2(math.e) / math.sqrt(queries.shape[-1])
    key_slot = lax.broadcasted_iota(jnp.int32, (BLK, BLK), 0)
    query_slot = lax.broadcasted_iota(jnp.int32, (BLK, BLK), 1)
    blocked = key_slot > query_slot

    def one_block(source, carry):
        block = 2 * source + side
        own = prefix + block
        listed = [own - 2, own - 1, own, 0, 1] + [rand[block, column] for column in range(3)]
        chosen_keys = jnp.concatenate([keys[key_block] for key_block in listed], axis=0)
        chosen_values = jnp.concatenate([values[key_block] for key_block in listed], axis=1)
        scores = lax.dot_general(
            chosen_keys, queries[source, 0, 0], (((1,), (1,)), ((), ())), preferred_element_type=jnp.float32
        )
        diagonal = jnp.where(blocked, -jnp.inf, scores[2 * BLK : 3 * BLK])
        scores = jnp.concatenate([scores[: 2 * BLK], diagonal, scores[3 * BLK :]], axis=0)
        weights = jnp.exp2((scores - jnp.max(scores, axis=0, keepdims=True)) * factor)
        inverse = 1.0 / jnp.sum(weights, axis=0, keepdims=True)
        probs = (weights * inverse).astype(jnp.bfloat16)
        total = jnp.dot(chosen_values, probs, preferred_element_type=jnp.float32)
        out[source, 0] = total.T.astype(out.dtype)
        return carry

    lax.fori_loop(0, sources, one_block, 0, unroll=8 if sources % 8 == 0 else 1)


def attend(place, rand, parts, caches, first):
    sources, _, heads, _, width = parts[0][0].shape
    cached_rows = caches[0].shape[1]
    key_blocks = 2 * cached_rows // BLK + 2 * sources
    cache_spec = pl.BlockSpec((1, cached_rows, width), lambda head, *_: (first + head, 0, 0))

    def part_spec(index):
        return pl.BlockSpec((sources, 1, 1, BLK, width), lambda head, *_: (0, index, head, 0, 0))

    work = heads * sources * BLK * LISTED * BLK
    return pl.pallas_call(
        attention_kernel,
        grid_spec=pltpu.PrefetchScalarGridSpec(
            num_scalar_prefetch=2,
            grid=(heads,),
            in_specs=[part_spec(index) for _, index in parts] + [cache_spec] * 4,
            out_specs=pl.BlockSpec((sources, 1, BLK, width), lambda head, *_: (0, head, 0, 0)),
            scratch_shapes=[
                pltpu.VMEM((key_blocks, BLK, width), jnp.bfloat16),
                pltpu.VMEM((key_blocks, width, BLK), jnp.bfloat16),
            ],
        ),
        out_shape=jax.ShapeDtypeStruct((sources, heads, BLK, width), jnp.bfloat16),
        compiler_params=pltpu.CompilerParams(vmem_limit_bytes=48 * 1024 * 1024),
        cost_estimate=pl.CostEstimate(
            flops=4 * work * width,
            bytes_accessed=2 * heads * width * BLK * (6 * sources + 2 * key_blocks),
            transcendentals=work,
        ),
    )(place, rand, *[array for array, _ in parts], *caches)


def move(stage, groups, arrivals, departures):
    inward, outward = [], []
    for index, (sources, target) in enumerate(groups):
        slot = stage.at[index]
        inward.append(
            [
                pltpu.make_async_copy(source, slot.at[part], arrivals.at[index, part])
                for part, source in enumerate(sources)
            ]
        )
        outward.append(pltpu.make_async_copy(slot, target, departures.at[index]))
    for group in inward:
        for copy in group:
            copy.start()
    for group, departure in zip(inward, outward):
        for copy in group:
            copy.wait()
        departure.start()
    for departure in outward:
        departure.wait()


def move_call(kernel, stage, shape, place, *arrays, into=None):
    inputs = list(arrays) + ([] if into is None else [into])
    return pl.pallas_call(
        kernel,
        grid_spec=pltpu.PrefetchScalarGridSpec(
            num_scalar_prefetch=1,
            grid=(1,),
            in_specs=[pl.BlockSpec(memory_space=pl.ANY)] * len(inputs),
            out_specs=pl.BlockSpec(memory_space=pl.ANY),
            scratch_shapes=[
                pltpu.VMEM(stage, jnp.bfloat16),
                pltpu.SemaphoreType.DMA(stage[:2]),
                pltpu.SemaphoreType.DMA(stage[:1]),
            ],
        ),
        out_shape=jax.ShapeDtypeStruct(shape, jnp.bfloat16),
        input_output_aliases={} if into is None else {len(inputs): 0},
        compiler_params=pltpu.CompilerParams(vmem_limit_bytes=PACK_VMEM),
        cost_estimate=pl.CostEstimate(flops=0, bytes_accessed=4 * math.prod(stage), transcendentals=0),
    )(place, *inputs)


def pack(place, queries, stretch_keys, stretch_values, chunk, part):
    owners, _, local_rows, width = queries.shape
    heads = pl.ds(part * chunk, chunk)

    def kernel(place, queries, keys, values, out, stage, arrivals, departures):
        rows = pl.ds(place[0] * local_rows, local_rows)
        groups = [
            ((queries.at[owner, heads], keys.at[owner, heads, rows], values.at[owner, heads, rows]), out.at[owner])
            for owner in range(owners)
        ]
        move(stage, groups, arrivals, departures)

    shape = (owners, 3, chunk, local_rows, width)
    return move_call(kernel, shape, shape, place, queries, stretch_keys, stretch_values)


def collect(place, returned, owned, part, into):
    owners, chunk, local_rows, width = returned.shape
    heads = pl.ds(part * chunk, chunk)

    def kernel(place, returned, *refs):
        out, stage, arrivals, departures = refs[-4:]
        groups = [((returned.at[owner],), out.at[pl.ds(owner, 1), heads]) for owner in range(owners)]
        move(stage, groups, arrivals, departures)

    shape = (owners, owned, local_rows, width)
    return move_call(kernel, (owners, 1, chunk, local_rows, width), shape, place, returned, into=into)


def after(value, *earlier):
    return lax.optimization_barrier((value, *earlier))[0]


def per_device(queries, stretch_keys, stretch_values, cache_keys, cache_values, rand_blocks):
    heads, local_rows, width = queries.shape
    seq_devices = lax.axis_size("seq")
    side = lax.axis_index("cache")
    owned = heads // seq_devices
    swap = [(0, 1), (1, 0)]
    assert local_rows == BLK and lax.axis_size("cache") == 2

    def by_owner(rows):
        return rows.reshape(seq_devices, owned, rows.shape[1], width)

    def exchange(value):
        return lax.all_to_all(value, "seq", split_axis=0, concat_axis=0, tiled=True)

    place = jnp.reshape(side, (1,)).astype(jnp.int32)
    chunk = max(1, owned // 2)
    messages = [
        pack(place, by_owner(queries), by_owner(stretch_keys), by_owner(stretch_values), chunk, part)
        for part in range(owned // chunk)
    ]
    caches = (
        cache_keys,
        lax.ppermute(cache_keys, "cache", swap),
        cache_values,
        lax.ppermute(cache_values, "cache", swap),
    )
    result = attended = None
    for part, message in enumerate(messages):
        mine = exchange(message)
        if attended is not None:
            mine = after(mine, attended)
        theirs = lax.ppermute(mine, "cache", swap)
        parts = [(mine, 0), (mine, 1), (mine, 2), (theirs, 1), (theirs, 2)]
        attended = attend(place, rand_blocks, parts, caches, part * chunk)
        result = collect(place, exchange(attended), owned, part, result)
    return result.reshape(heads, local_rows, width)


def solution(mesh):
    placed = (
        P("groups", ("seq", "cache"), None),
        P("groups", "seq", None),
        P("groups", "seq", None),
        P(("groups", "seq"), "cache", None),
        P(("groups", "seq"), "cache", None),
        P("groups", None),
    )
    return jax.shard_map(
        per_device,
        mesh=mesh,
        in_specs=placed,
        out_specs=P("groups", ("seq", "cache"), None),
        check_vma=False,
    )
```

```python
import math

import jax
import jax.numpy as jnp
from jax import lax
from jax.experimental import pallas as pl
from jax.experimental.pallas import tpu as pltpu
from jax.sharding import PartitionSpec as P

BLK = 128
LISTED = 8
UNROLL = 16
OWNED = 4
EARLY = 3


def unroll_of(sources):
    return UNROLL if sources % UNROLL == 0 else 1


def listed_blocks(rand, prefix, block):
    own = prefix + block
    return [own - 2, own - 1, own, 0, 1] + [rand[block, column] for column in range(3)]


def fill(blocks, side, cached_mine, cached_theirs, sources, put):
    cached = cached_mine.shape[1] // BLK
    for index in range(cached):
        rows = pl.ds(index * BLK, BLK)
        blocks[side * cached + index] = put(cached_mine[0, rows, :])
        blocks[(1 - side) * cached + index] = put(cached_theirs[0, rows, :])
    for block, ref, index in sources:
        blocks[2 * cached + block] = put(ref[index, 0])


def turned(block):
    return block.T


def same(block):
    return block


def probabilities(query, keys, listed):
    factor = math.log2(math.e) / math.sqrt(query.shape[-1])
    key_slot = lax.broadcasted_iota(jnp.int32, (BLK, BLK), 0)
    query_slot = lax.broadcasted_iota(jnp.int32, (BLK, BLK), 1)
    chosen = jnp.concatenate([keys[key_block] for key_block in listed], axis=0)
    scores = lax.dot_general(chosen, query, (((1,), (1,)), ((), ())), preferred_element_type=jnp.float32)
    diagonal = jnp.where(key_slot > query_slot, -jnp.inf, scores[2 * BLK : 3 * BLK])
    scores = jnp.concatenate([scores[: 2 * BLK], diagonal, scores[3 * BLK :]], axis=0)
    weights = jnp.exp2((scores - jnp.max(scores, axis=0, keepdims=True)) * factor)
    inverse = 1.0 / jnp.sum(weights, axis=0, keepdims=True)
    return (weights * inverse).astype(jnp.bfloat16)


def weighted(probs, values, listed):
    chosen = jnp.concatenate([values[key_block] for key_block in listed], axis=1)
    return jnp.dot(chosen, probs, preferred_element_type=jnp.float32).T.astype(jnp.bfloat16)


def attention_kernel(paired, place, rand, queries, keys_mine, values_mine, ck_mine, ck_theirs, cv_mine, cv_theirs, *refs):
    theirs = refs[:2] if paired else None
    out, keys, values = refs[-3:]
    sources = queries.shape[0]
    prefix = 2 * ck_mine.shape[1] // BLK
    side = place[0]

    def block_of(source, which):
        return 2 * source + which if paired else source

    def rows_of(mine, part):
        rows = [(block_of(source, side), mine, source) for source in range(sources)]
        if paired:
            rows += [(block_of(source, 1 - side), theirs[part], source) for source in range(sources)]
        return rows

    fill(keys, side, ck_mine, ck_theirs, rows_of(keys_mine, 0), same)
    fill(values, side, cv_mine, cv_theirs, rows_of(values_mine, 1), turned)

    def one_block(source, carry):
        listed = listed_blocks(rand, prefix, block_of(source, side))
        out[source, 0] = weighted(probabilities(queries[source, 0], keys, listed), values, listed)
        return carry

    lax.fori_loop(0, sources, one_block, 0, unroll=unroll_of(sources))


def attend(place, rand, mine, theirs, caches, owned, first=0, into=None):
    sources, slabs, _, width = mine.shape
    heads = slabs // 3
    paired = theirs is not None
    cached_rows = caches[0].shape[1]
    key_blocks = 2 * cached_rows // BLK + (2 if paired else 1) * sources

    def slab(part):
        return pl.BlockSpec((sources, 1, BLK, width), lambda head, *_: (0, part * heads + head, 0, 0))

    def cache_index(head, place, rand):
        return ((0 if paired else place[0] * owned) + first + head, 0, 0)

    arrays = [in_hbm(array) for array in [mine] * 3 + list(caches) + ([theirs] * 2 if paired else [])]
    in_specs = [slab(0), slab(1), slab(2)] + [pl.BlockSpec((1, cached_rows, width), cache_index)] * 4
    in_specs += [slab(1), slab(2)] if paired else []
    aliases = {}
    if into is not None:
        aliases = {2 + len(arrays): 0}
        arrays.append(into)
        in_specs.append(pl.BlockSpec(memory_space=pl.ANY))
    work = heads * sources * BLK * LISTED * BLK
    return pl.pallas_call(
        lambda *refs: attention_kernel(paired, *refs),
        grid_spec=pltpu.PrefetchScalarGridSpec(
            num_scalar_prefetch=2,
            grid=(heads,),
            in_specs=in_specs,
            out_specs=pl.BlockSpec((sources, 1, BLK, width), lambda head, *_: (0, first + head, 0, 0)),
            scratch_shapes=[
                pltpu.VMEM((key_blocks, BLK, width), jnp.bfloat16),
                pltpu.VMEM((key_blocks, width, BLK), jnp.bfloat16),
            ],
        ),
        out_shape=jax.ShapeDtypeStruct((sources, owned, BLK, width), jnp.bfloat16),
        input_output_aliases=aliases,
        compiler_params=pltpu.CompilerParams(vmem_limit_bytes=48 * 1024 * 1024),
        cost_estimate=pl.CostEstimate(
            flops=4 * work * width,
            bytes_accessed=2 * heads * width * BLK * (4 * sources + 2 * key_blocks),
            transcendentals=work,
        ),
    )(place, rand, *arrays)


def in_hbm(array):
    return pltpu.with_memory_space_constraint(array, pltpu.HBM)


def pack(place, arrays, plan):
    owners, _, local_rows, width = arrays[0].shape
    slabs = sum(count for _, _, count in plan)
    group = 4 if owners % 4 == 0 else 1

    def kernel(place, *refs):
        sources, (out, stage, arrivals, departures) = refs[:-4], refs[-4:]
        rows = pl.ds(place[0] * local_rows, local_rows)
        inward = []
        for owner in range(owners):
            slab = 0
            for part, (index, first, count) in enumerate(plan):
                heads, whole = pl.ds(first, count), sources[index].shape[2] == local_rows
                source = sources[index].at[owner, heads] if whole else sources[index].at[owner, heads, rows]
                target = stage.at[owner, pl.ds(slab, count)]
                inward.append(pltpu.make_async_copy(source, target, arrivals.at[owner, part]))
                slab += count
        outward = []
        for index in range(owners // group):
            some = pl.ds(index * group, group)
            outward.append(pltpu.make_async_copy(stage.at[some], out.at[some], departures.at[index]))
        for copy in inward:
            copy.start()
        for index, departure in enumerate(outward):
            for copy in inward[index * group * len(plan) : (index + 1) * group * len(plan)]:
                copy.wait()
            departure.start()
        for departure in outward:
            departure.wait()

    shape = (owners, slabs, local_rows, width)
    return pl.pallas_call(
        kernel,
        grid_spec=pltpu.PrefetchScalarGridSpec(
            num_scalar_prefetch=1,
            grid=(1,),
            in_specs=[pl.BlockSpec(memory_space=pltpu.HBM)] * len(arrays),
            out_specs=pl.BlockSpec(memory_space=pltpu.HBM),
            scratch_shapes=[
                pltpu.VMEM(shape, jnp.bfloat16),
                pltpu.SemaphoreType.DMA((owners, len(plan))),
                pltpu.SemaphoreType.DMA((owners // group,)),
            ],
        ),
        out_shape=pltpu.HBM(shape, jnp.bfloat16),
        compiler_params=pltpu.CompilerParams(vmem_limit_bytes=48 * 1024 * 1024),
        cost_estimate=pl.CostEstimate(flops=0, bytes_accessed=4 * math.prod(shape), transcendentals=0),
    )(place, *[in_hbm(array) for array in arrays])


def after(value, *earlier):
    return lax.optimization_barrier((value, *earlier))[0]


def per_device(queries, stretch_keys, stretch_values, cache_keys, cache_values, rand_blocks):
    heads, local_rows, width = queries.shape
    side = lax.axis_index("cache")
    assert local_rows == BLK and lax.axis_size("cache") == 2
    place = jnp.reshape(side, (1,)).astype(jnp.int32)

    def to_sibling(value):
        return lax.ppermute(value, "cache", [(0, 1), (1, 0)])

    by_heads = heads % (2 * lax.axis_size("seq")) == 0
    axes = ("seq", "cache") if by_heads else "seq"
    owners = lax.axis_size(axes)
    owned = heads // owners
    arrays = [rows.reshape(owners, owned, rows.shape[1], width) for rows in (queries, stretch_keys, stretch_values)]
    caches = (cache_keys, to_sibling(cache_keys), cache_values, to_sibling(cache_values))

    def exchange(value):
        return lax.all_to_all(value, axes, split_axis=0, concat_axis=0, tiled=True)

    splits = [(0, EARLY), (EARLY, owned - EARLY)] if by_heads and owned == OWNED else [(0, owned)]
    attended = None
    for first, count in splits:
        mine = exchange(pack(place, arrays, [(index, first, count) for index in range(3)]))
        if attended is not None:
            mine = after(mine, attended)
        theirs = None if by_heads else to_sibling(mine)
        attended = attend(place, rand_blocks, mine, theirs, caches, owned, first, attended)
    return exchange(attended).reshape(heads, local_rows, width)


def solution(mesh):
    placed = (
        P("groups", ("seq", "cache"), None),
        P("groups", "seq", None),
        P("groups", "seq", None),
        P(("groups", "seq"), "cache", None),
        P(("groups", "seq"), "cache", None),
        P("groups", None),
    )
    return jax.shard_map(
        per_device,
        mesh=mesh,
        in_specs=placed,
        out_specs=P("groups", ("seq", "cache"), None),
        check_vma=False,
    )
```

```python
import math

import jax
import jax.numpy as jnp
from jax import lax
from jax.experimental import pallas as pl
from jax.experimental.pallas import tpu as pltpu
from jax.sharding import PartitionSpec as P

BLK = 128
LISTED = 8
UNROLL = 16
OWNED = 4
EARLY = 2
WINDOW = 5
GATE = 6
STEPS = (0, 8, 1, 9, 2, 10, 3, 11, 4, 12, 5, 13, 6, 14, 7, 15)


def unroll_of(sources):
    return UNROLL if sources % UNROLL == 0 else 1


def listed_blocks(rand, prefix, block):
    own = prefix + block
    return [own - 2, own - 1, own, 0, 1] + [rand[block, column] for column in range(3)]


def fill(blocks, side, cached_mine, cached_theirs, sources, put):
    cached = cached_mine.shape[1] // BLK
    for index in range(cached):
        rows = pl.ds(index * BLK, BLK)
        blocks[side * cached + index] = put(cached_mine[0, rows, :])
        blocks[(1 - side) * cached + index] = put(cached_theirs[0, rows, :])
    for block, ref, index in sources:
        blocks[2 * cached + block] = put(ref[index])


def turned(block):
    return block.T


def same(block):
    return block


def probabilities(query, keys, listed):
    factor = math.log2(math.e) / math.sqrt(query.shape[-1])
    key_slot = lax.broadcasted_iota(jnp.int32, (BLK, BLK), 0)
    query_slot = lax.broadcasted_iota(jnp.int32, (BLK, BLK), 1)
    chosen = jnp.concatenate([keys[key_block] for key_block in listed], axis=0)
    scores = lax.dot_general(chosen, query, (((1,), (1,)), ((), ())), preferred_element_type=jnp.float32)
    diagonal = jnp.where(key_slot > query_slot, -jnp.inf, scores[2 * BLK : 3 * BLK])
    scores = jnp.concatenate([scores[: 2 * BLK], diagonal, scores[3 * BLK :]], axis=0)
    weights = jnp.exp2((scores - jnp.max(scores, axis=0, keepdims=True)) * factor)
    inverse = 1.0 / jnp.sum(weights, axis=0, keepdims=True)
    return (weights * inverse).astype(jnp.bfloat16)


def weighted(probs, values, listed):
    chosen = jnp.concatenate([values[key_block] for key_block in listed], axis=1)
    return jnp.dot(chosen, probs, preferred_element_type=jnp.float32).T.astype(jnp.bfloat16)


def attention_kernel(paired, place, rand, queries, keys_mine, values_mine, ck_mine, ck_theirs, cv_mine, cv_theirs, *refs):
    theirs = refs[:2] if paired else None
    out, keys, values = refs[-3:]
    sources = queries.shape[0]
    prefix = 2 * ck_mine.shape[1] // BLK
    side = place[0]

    def block_of(source, which):
        return 2 * source + which if paired else source

    def rows_of(mine, part):
        rows = [(block_of(source, side), mine, (source, 0)) for source in range(sources)]
        if paired:
            rows += [(block_of(source, 1 - side), theirs[part], (source, 0)) for source in range(sources)]
        return rows

    fill(keys, side, ck_mine, ck_theirs, rows_of(keys_mine, 0), same)
    fill(values, side, cv_mine, cv_theirs, rows_of(values_mine, 1), turned)

    def one_block(source, carry):
        listed = listed_blocks(rand, prefix, block_of(source, side))
        out[source, 0] = weighted(probabilities(queries[source, 0], keys, listed), values, listed)
        return carry

    lax.fori_loop(0, sources, one_block, 0, unroll=unroll_of(sources))


def attend(place, rand, mine, theirs, caches, owned):
    sources, slabs, _, width = mine.shape
    heads = slabs // 3
    paired = theirs is not None
    cached_rows = caches[0].shape[1]
    key_blocks = 2 * cached_rows // BLK + (2 if paired else 1) * sources

    def slab(part):
        return pl.BlockSpec((sources, 1, BLK, width), lambda head, *_: (0, part * heads + head, 0, 0))

    def cache_index(head, place, rand):
        return ((0 if paired else place[0] * owned) + head, 0, 0)

    arrays = [in_hbm(array) for array in [mine] * 3 + list(caches) + ([theirs] * 2 if paired else [])]
    in_specs = [slab(0), slab(1), slab(2)] + [pl.BlockSpec((1, cached_rows, width), cache_index)] * 4
    in_specs += [slab(1), slab(2)] if paired else []
    work = heads * sources * BLK * LISTED * BLK
    return pl.pallas_call(
        lambda *refs: attention_kernel(paired, *refs),
        grid_spec=pltpu.PrefetchScalarGridSpec(
            num_scalar_prefetch=2,
            grid=(heads,),
            in_specs=in_specs,
            out_specs=pl.BlockSpec((sources, 1, BLK, width), lambda head, *_: (0, head, 0, 0)),
            scratch_shapes=[
                pltpu.VMEM((key_blocks, BLK, width), jnp.bfloat16),
                pltpu.VMEM((key_blocks, width, BLK), jnp.bfloat16),
            ],
        ),
        out_shape=jax.ShapeDtypeStruct((sources, owned, BLK, width), jnp.bfloat16),
        compiler_params=pltpu.CompilerParams(vmem_limit_bytes=48 * 1024 * 1024),
        cost_estimate=pl.CostEstimate(
            flops=4 * work * width,
            bytes_accessed=2 * heads * width * BLK * (4 * sources + 2 * key_blocks),
            transcendentals=work,
        ),
    )(place, rand, *arrays)


def pieces_kernel(pieces, by_step, place, rand, *refs):
    mine, (ck_mine, ck_theirs, cv_mine, cv_theirs) = refs[:pieces], refs[pieces : pieces + 4]
    keys, values, queries, results = refs[-4:]
    outs = refs[pieces + 4 : -4]
    prefix = 2 * ck_mine.shape[1] // BLK
    side = place[0]
    rows = [(place[1 + index], ref) for index, ref in enumerate(mine)]
    fill(keys, side, ck_mine, ck_theirs, [(source, ref, (0, 0, 1)) for source, ref in rows], same)
    fill(values, side, cv_mine, cv_theirs, [(source, ref, (0, 0, 2)) for source, ref in rows], turned)
    for source, ref in rows:
        queries[source] = ref[0, 0, 0]

    def one_block(source, carry):
        listed = listed_blocks(rand, prefix, source)
        results[source] = weighted(probabilities(queries[source], keys, listed), values, listed)
        return carry

    lax.fori_loop(0, pieces, one_block, 0, unroll=unroll_of(pieces))
    if by_step:
        for index, out in enumerate(outs):
            out[0, 0] = results[place[1 + pieces + index]]
    else:
        outs[0][:, 0] = results[...]


def attend_pieces(place, rand, mine, caches, owned, first, by_step=False):
    pieces = len(mine)
    _, heads, _, _, width = mine[0].shape
    cached_rows = caches[0].shape[1]
    key_blocks = 2 * cached_rows // BLK + pieces
    piece_spec = pl.BlockSpec((1, 1, 3, BLK, width), lambda head, *_: (0, head, 0, 0, 0))
    cache_spec = pl.BlockSpec((1, cached_rows, width), lambda head, place, rand: (place[0] * owned + first + head, 0, 0))
    arrays = [in_hbm(array) for array in [*mine, *caches]]
    in_specs = [piece_spec] * pieces + [cache_spec] * 4
    outs = pieces if by_step else 1
    work = heads * pieces * BLK * LISTED * BLK
    return pl.pallas_call(
        lambda *refs: pieces_kernel(pieces, by_step, *refs),
        grid_spec=pltpu.PrefetchScalarGridSpec(
            num_scalar_prefetch=2,
            grid=(heads,),
            in_specs=in_specs,
            out_specs=[pl.BlockSpec((pieces // outs, 1, BLK, width), lambda head, *_: (0, head, 0, 0))] * outs,
            scratch_shapes=[
                pltpu.VMEM((key_blocks, BLK, width), jnp.bfloat16),
                pltpu.VMEM((key_blocks, width, BLK), jnp.bfloat16),
                pltpu.VMEM((pieces, BLK, width), jnp.bfloat16),
                pltpu.VMEM((pieces, BLK, width), jnp.bfloat16),
            ],
        ),
        out_shape=[jax.ShapeDtypeStruct((pieces // outs, heads, BLK, width), jnp.bfloat16)] * outs,
        compiler_params=pltpu.CompilerParams(vmem_limit_bytes=48 * 1024 * 1024),
        cost_estimate=pl.CostEstimate(
            flops=24 * work * width,
            bytes_accessed=2 * heads * width * BLK * (4 * pieces + 2 * key_blocks),
            transcendentals=work,
        ),
    )(place, rand, *arrays)


def in_hbm(array):
    return pltpu.with_memory_space_constraint(array, pltpu.HBM)


def pack(place, arrays, plan):
    owners, _, local_rows, width = arrays[0].shape
    slabs = sum(count for _, _, count in plan)
    group = 4 if owners % 4 == 0 else 1

    def kernel(place, *refs):
        sources, (out, stage, arrivals, departures) = refs[:-4], refs[-4:]
        rows = pl.ds(place[0] * local_rows, local_rows)
        inward = []
        for owner in range(owners):
            slab = 0
            for part, (index, first, count) in enumerate(plan):
                heads, whole = pl.ds(first, count), sources[index].shape[2] == local_rows
                source = sources[index].at[owner, heads] if whole else sources[index].at[owner, heads, rows]
                target = stage.at[owner, pl.ds(slab, count)]
                inward.append(pltpu.make_async_copy(source, target, arrivals.at[owner, part]))
                slab += count
        outward = []
        for index in range(owners // group):
            some = pl.ds(index * group, group)
            outward.append(pltpu.make_async_copy(stage.at[some], out.at[some], departures.at[index]))
        for copy in inward:
            copy.start()
        for index, departure in enumerate(outward):
            for copy in inward[index * group * len(plan) : (index + 1) * group * len(plan)]:
                copy.wait()
            departure.start()
        for departure in outward:
            departure.wait()

    shape = (owners, slabs, local_rows, width)
    return pl.pallas_call(
        kernel,
        grid_spec=pltpu.PrefetchScalarGridSpec(
            num_scalar_prefetch=1,
            grid=(1,),
            in_specs=[pl.BlockSpec(memory_space=pltpu.HBM)] * len(arrays),
            out_specs=pl.BlockSpec(memory_space=pltpu.HBM),
            scratch_shapes=[
                pltpu.VMEM(shape, jnp.bfloat16),
                pltpu.SemaphoreType.DMA((owners, len(plan))),
                pltpu.SemaphoreType.DMA((owners // group,)),
            ],
        ),
        out_shape=pltpu.HBM(shape, jnp.bfloat16),
        compiler_params=pltpu.CompilerParams(vmem_limit_bytes=48 * 1024 * 1024),
        cost_estimate=pl.CostEstimate(flops=0, bytes_accessed=4 * math.prod(shape), transcendentals=0),
    )(place, *[in_hbm(array) for array in arrays])


def pack_each(place, arrays, steps, first, count):
    _, _, local_rows, width = arrays[0].shape
    heads = pl.ds(first, count)
    parts = len(arrays)

    def kernel(place, *refs):
        sources, outs, (stage, arrivals, departures) = refs[:parts], refs[parts:-3], refs[-3:]
        rows = pl.ds(place[0] * local_rows, local_rows)
        inward, outward = [], []
        for index, step in enumerate(steps):
            owner = place[1 + step]
            for part, source in enumerate(sources):
                piece = source.at[owner, heads] if source.shape[2] == local_rows else source.at[owner, heads, rows]
                inward.append(pltpu.make_async_copy(piece, stage.at[index, :, part], arrivals.at[index, part]))
            outward.append(pltpu.make_async_copy(stage.at[index], outs[index].at[0], departures.at[index]))
        for copy in inward:
            copy.start()
        for index, departure in enumerate(outward):
            for copy in inward[index * parts : (index + 1) * parts]:
                copy.wait()
            departure.start()
        for departure in outward:
            departure.wait()

    shape = (count, parts, local_rows, width)
    return pl.pallas_call(
        kernel,
        grid_spec=pltpu.PrefetchScalarGridSpec(
            num_scalar_prefetch=1,
            grid=(1,),
            in_specs=[pl.BlockSpec(memory_space=pltpu.HBM)] * parts,
            out_specs=[pl.BlockSpec(memory_space=pltpu.HBM)] * len(steps),
            scratch_shapes=[
                pltpu.VMEM((len(steps),) + shape, jnp.bfloat16),
                pltpu.SemaphoreType.DMA((len(steps), parts)),
                pltpu.SemaphoreType.DMA((len(steps),)),
            ],
        ),
        out_shape=[pltpu.HBM((1,) + shape, jnp.bfloat16)] * len(steps),
        compiler_params=pltpu.CompilerParams(vmem_limit_bytes=48 * 1024 * 1024),
        cost_estimate=pl.CostEstimate(flops=0, bytes_accessed=4 * len(steps) * math.prod(shape), transcendentals=0),
    )(place, *[in_hbm(array) for array in arrays])


def collect(place, returned, owned, first, into=None):
    apart = isinstance(returned, list)
    arrays = returned if apart else [returned]
    owners = len(arrays) if apart else returned.shape[0]
    _, count, local_rows, width = arrays[0].shape
    heads = pl.ds(first, count)
    arrays = [in_hbm(array) for array in arrays] + ([] if into is None else [into])

    def kernel(place, *refs):
        sources, (out, stage, arrivals, departures) = refs[:-4], refs[-4:]
        inward, outward = [], []
        for index in range(owners):
            source = sources[index].at[0] if apart else sources[0].at[index]
            owner = place[1 + index] if apart else index
            inward.append(pltpu.make_async_copy(source, stage.at[index], arrivals.at[index]))
            outward.append(pltpu.make_async_copy(stage.at[index], out.at[owner, heads], departures.at[index]))
        for copy in inward:
            copy.start()
        for copy, departure in zip(inward, outward):
            copy.wait()
            departure.start()
        for departure in outward:
            departure.wait()

    return pl.pallas_call(
        kernel,
        grid_spec=pltpu.PrefetchScalarGridSpec(
            num_scalar_prefetch=1,
            grid=(1,),
            in_specs=[pl.BlockSpec(memory_space=pl.ANY)] * len(arrays),
            out_specs=pl.BlockSpec(memory_space=pl.ANY),
            scratch_shapes=[
                pltpu.VMEM((owners, count, local_rows, width), jnp.bfloat16),
                pltpu.SemaphoreType.DMA((owners,)),
                pltpu.SemaphoreType.DMA((owners,)),
            ],
        ),
        out_shape=jax.ShapeDtypeStruct((owners, owned, local_rows, width), jnp.bfloat16),
        input_output_aliases={} if into is None else {len(arrays): 0},
        compiler_params=pltpu.CompilerParams(vmem_limit_bytes=48 * 1024 * 1024),
        cost_estimate=pl.CostEstimate(
            flops=0, bytes_accessed=4 * owners * count * local_rows * width, transcendentals=0
        ),
    )(place, *arrays)


def after(value, *earlier):
    return lax.optimization_barrier((value, *earlier))[0]


def per_device(queries, stretch_keys, stretch_values, cache_keys, cache_values, rand_blocks):
    heads, local_rows, width = queries.shape
    side = lax.axis_index("cache")
    assert local_rows == BLK and lax.axis_size("cache") == 2
    place = jnp.reshape(side, (1,)).astype(jnp.int32)

    def to_sibling(value):
        return lax.ppermute(value, "cache", [(0, 1), (1, 0)])

    by_heads = heads % (2 * lax.axis_size("seq")) == 0
    axes = ("seq", "cache") if by_heads else "seq"
    owners = lax.axis_size(axes)
    owned = heads // owners
    arrays = [rows.reshape(owners, owned, rows.shape[1], width) for rows in (queries, stretch_keys, stretch_values)]
    caches = (cache_keys, to_sibling(cache_keys), cache_values, to_sibling(cache_values))

    def exchange(value):
        return lax.all_to_all(value, axes, split_axis=0, concat_axis=0, tiled=True)

    if owners != 16 or owned != OWNED:
        mine = exchange(pack(place, arrays, [(index, 0, owned) for index in range(3)]))
        theirs = None if by_heads else to_sibling(mine)
        attended = attend(place, rand_blocks, mine, theirs, caches, owned)
        return exchange(attended).reshape(heads, local_rows, width)

    here = 2 * lax.axis_index("seq") + side
    owner_at = jnp.stack([side] + [here ^ step ^ (8 * side) for step in range(owners)]).astype(jnp.int32)
    source_at = jnp.stack([side] + [here ^ step ^ (8 * (side ^ (step & 1))) for step in range(owners)]).astype(jnp.int32)
    sent = []

    def pairs_of(step):
        return [(index, index ^ step ^ (8 * (index & 1))) for index in range(owners)]

    def send(message, step):
        if len(sent) >= WINDOW:
            message = after(message, sent[-WINDOW])
        sent.append(lax.ppermute(message, axes, pairs_of(step)))
        return sent[-1]

    early, late = [None] * owners, [None] * owners
    for step, message in zip(STEPS, pack_each(owner_at, arrays, STEPS, 0, EARLY)):
        early[step] = send(message, step)
    messages = pack_each(owner_at, arrays, STEPS, EARLY, owned - EARLY)
    both = jnp.concatenate([source_at, owner_at[1:]])
    attended = attend_pieces(both, rand_blocks, early, caches, owned, 0)[0]
    for index, (step, message) in enumerate(zip(STEPS, messages)):
        late[step] = send(message if index < GATE else after(message, attended), step)
    attended = after(attended, *late)
    taken = exchange(attended)
    result = collect(source_at, taken, owned, 0)
    parts = attend_pieces(both, rand_blocks, late, caches, owned, EARLY, True)
    returned = [None] * owners
    for index, step in enumerate(STEPS):
        returned[step] = lax.ppermute(parts[step], axes, pairs_of(step))
    result = collect(source_at, returned, owned, EARLY, result)
    return result.reshape(heads, local_rows, width)


def solution(mesh):
    placed = (
        P("groups", ("seq", "cache"), None),
        P("groups", "seq", None),
        P("groups", "seq", None),
        P(("groups", "seq"), "cache", None),
        P(("groups", "seq"), "cache", None),
        P("groups", None),
    )
    return jax.shard_map(
        per_device,
        mesh=mesh,
        in_specs=placed,
        out_specs=P("groups", ("seq", "cache"), None),
        check_vma=False,
    )
```

```python
import math

import jax
import jax.numpy as jnp
from jax import lax
from jax.experimental import pallas as pl
from jax.experimental.pallas import tpu as pltpu
from jax.sharding import PartitionSpec as P

BLK = 128
LISTED = 8
UNROLL = 16
OWNED = 4
EARLY = 2
WINDOW = 5
GATE = 5
STEPS = (0, 8, 1, 9, 2, 10, 3, 11, 4, 12, 5, 13, 6, 14, 7, 15)


def unroll_of(sources):
    return UNROLL if sources % UNROLL == 0 else 1


def listed_blocks(rand, prefix, block):
    own = prefix + block
    return [own - 2, own - 1, own, 0, 1] + [rand[block, column] for column in range(3)]


def fill(blocks, side, cached_mine, cached_theirs, sources, put):
    cached = cached_mine.shape[1] // BLK
    for index in range(cached):
        rows = pl.ds(index * BLK, BLK)
        blocks[side * cached + index] = put(cached_mine[0, rows, :])
        blocks[(1 - side) * cached + index] = put(cached_theirs[0, rows, :])
    for block, ref, index in sources:
        blocks[2 * cached + block] = put(ref[index])


def turned(block):
    return block.T


def same(block):
    return block


def probabilities(query, keys, listed):
    factor = math.log2(math.e) / math.sqrt(query.shape[-1])
    key_slot = lax.broadcasted_iota(jnp.int32, (BLK, BLK), 0)
    query_slot = lax.broadcasted_iota(jnp.int32, (BLK, BLK), 1)
    chosen = jnp.concatenate([keys[key_block] for key_block in listed], axis=0)
    scores = lax.dot_general(chosen, query, (((1,), (1,)), ((), ())), preferred_element_type=jnp.float32)
    diagonal = jnp.where(key_slot > query_slot, -jnp.inf, scores[2 * BLK : 3 * BLK])
    scores = jnp.concatenate([scores[: 2 * BLK], diagonal, scores[3 * BLK :]], axis=0)
    weights = jnp.exp2((scores - jnp.max(scores, axis=0, keepdims=True)) * factor)
    inverse = 1.0 / jnp.sum(weights, axis=0, keepdims=True)
    return (weights * inverse).astype(jnp.bfloat16)


def weighted(probs, values, listed):
    chosen = jnp.concatenate([values[key_block] for key_block in listed], axis=1)
    return jnp.dot(chosen, probs, preferred_element_type=jnp.float32).T.astype(jnp.bfloat16)


def attention_kernel(paired, place, rand, queries, keys_mine, values_mine, ck_mine, ck_theirs, cv_mine, cv_theirs, *refs):
    theirs = refs[:2] if paired else None
    out, keys, values = refs[-3:]
    sources = queries.shape[0]
    prefix = 2 * ck_mine.shape[1] // BLK
    side = place[0]

    def block_of(source, which):
        return 2 * source + which if paired else source

    def rows_of(mine, part):
        rows = [(block_of(source, side), mine, (source, 0)) for source in range(sources)]
        if paired:
            rows += [(block_of(source, 1 - side), theirs[part], (source, 0)) for source in range(sources)]
        return rows

    fill(keys, side, ck_mine, ck_theirs, rows_of(keys_mine, 0), same)
    fill(values, side, cv_mine, cv_theirs, rows_of(values_mine, 1), turned)

    def one_block(source, carry):
        listed = listed_blocks(rand, prefix, block_of(source, side))
        out[source, 0] = weighted(probabilities(queries[source, 0], keys, listed), values, listed)
        return carry

    lax.fori_loop(0, sources, one_block, 0, unroll=unroll_of(sources))


def attend(place, rand, mine, theirs, caches, owned):
    sources, slabs, _, width = mine.shape
    heads = slabs // 3
    paired = theirs is not None
    cached_rows = caches[0].shape[1]
    key_blocks = 2 * cached_rows // BLK + (2 if paired else 1) * sources

    def slab(part):
        return pl.BlockSpec((sources, 1, BLK, width), lambda head, *_: (0, part * heads + head, 0, 0))

    def cache_index(head, place, rand):
        return ((0 if paired else place[0] * owned) + head, 0, 0)

    arrays = [in_hbm(array) for array in [mine] * 3 + list(caches) + ([theirs] * 2 if paired else [])]
    in_specs = [slab(0), slab(1), slab(2)] + [pl.BlockSpec((1, cached_rows, width), cache_index)] * 4
    in_specs += [slab(1), slab(2)] if paired else []
    work = heads * sources * BLK * LISTED * BLK
    return pl.pallas_call(
        lambda *refs: attention_kernel(paired, *refs),
        grid_spec=pltpu.PrefetchScalarGridSpec(
            num_scalar_prefetch=2,
            grid=(heads,),
            in_specs=in_specs,
            out_specs=pl.BlockSpec((sources, 1, BLK, width), lambda head, *_: (0, head, 0, 0)),
            scratch_shapes=[
                pltpu.VMEM((key_blocks, BLK, width), jnp.bfloat16),
                pltpu.VMEM((key_blocks, width, BLK), jnp.bfloat16),
            ],
        ),
        out_shape=jax.ShapeDtypeStruct((sources, owned, BLK, width), jnp.bfloat16),
        compiler_params=pltpu.CompilerParams(vmem_limit_bytes=48 * 1024 * 1024),
        cost_estimate=pl.CostEstimate(
            flops=4 * work * width,
            bytes_accessed=2 * heads * width * BLK * (4 * sources + 2 * key_blocks),
            transcendentals=work,
        ),
    )(place, rand, *arrays)


def pieces_kernel(pieces, by_step, place, rand, *refs):
    mine, (ck_mine, ck_theirs, cv_mine, cv_theirs) = refs[:pieces], refs[pieces : pieces + 4]
    keys, values, queries, results = refs[-4:]
    outs = refs[pieces + 4 : -4]
    prefix = 2 * ck_mine.shape[1] // BLK
    side = place[0]
    rows = [(place[1 + index], ref) for index, ref in enumerate(mine)]
    fill(keys, side, ck_mine, ck_theirs, [(source, ref, (0, 0, 1)) for source, ref in rows], same)
    fill(values, side, cv_mine, cv_theirs, [(source, ref, (0, 0, 2)) for source, ref in rows], turned)
    for source, ref in rows:
        queries[source] = ref[0, 0, 0]

    def one_block(source, carry):
        listed = listed_blocks(rand, prefix, source)
        results[source] = weighted(probabilities(queries[source], keys, listed), values, listed)
        return carry

    lax.fori_loop(0, pieces, one_block, 0, unroll=unroll_of(pieces))
    if by_step:
        for index, out in enumerate(outs):
            out[0, 0] = results[place[1 + pieces + index]]
    else:
        outs[0][:, 0] = results[...]


def attend_pieces(place, rand, mine, caches, owned, first, by_step=False):
    pieces = len(mine)
    _, heads, _, _, width = mine[0].shape
    cached_rows = caches[0].shape[1]
    key_blocks = 2 * cached_rows // BLK + pieces
    piece_spec = pl.BlockSpec((1, 1, 3, BLK, width), lambda head, *_: (0, head, 0, 0, 0))
    cache_spec = pl.BlockSpec((1, cached_rows, width), lambda head, place, rand: (place[0] * owned + first + head, 0, 0))
    arrays = [in_hbm(array) for array in [*mine, *caches]]
    in_specs = [piece_spec] * pieces + [cache_spec] * 4
    outs = pieces if by_step else 1
    work = heads * pieces * BLK * LISTED * BLK
    return pl.pallas_call(
        lambda *refs: pieces_kernel(pieces, by_step, *refs),
        grid_spec=pltpu.PrefetchScalarGridSpec(
            num_scalar_prefetch=2,
            grid=(heads,),
            in_specs=in_specs,
            out_specs=[pl.BlockSpec((pieces // outs, 1, BLK, width), lambda head, *_: (0, head, 0, 0))] * outs,
            scratch_shapes=[
                pltpu.VMEM((key_blocks, BLK, width), jnp.bfloat16),
                pltpu.VMEM((key_blocks, width, BLK), jnp.bfloat16),
                pltpu.VMEM((pieces, BLK, width), jnp.bfloat16),
                pltpu.VMEM((pieces, BLK, width), jnp.bfloat16),
            ],
        ),
        out_shape=[jax.ShapeDtypeStruct((pieces // outs, heads, BLK, width), jnp.bfloat16)] * outs,
        compiler_params=pltpu.CompilerParams(vmem_limit_bytes=48 * 1024 * 1024),
        cost_estimate=pl.CostEstimate(
            flops=24 * work * width,
            bytes_accessed=2 * heads * width * BLK * (4 * pieces + 2 * key_blocks),
            transcendentals=work,
        ),
    )(place, rand, *arrays)


def in_hbm(array):
    return pltpu.with_memory_space_constraint(array, pltpu.HBM)


def pack(place, arrays, plan):
    owners, _, local_rows, width = arrays[0].shape
    slabs = sum(count for _, _, count in plan)
    group = 4 if owners % 4 == 0 else 1

    def kernel(place, *refs):
        sources, (out, stage, arrivals, departures) = refs[:-4], refs[-4:]
        rows = pl.ds(place[0] * local_rows, local_rows)
        inward = []
        for owner in range(owners):
            slab = 0
            for part, (index, first, count) in enumerate(plan):
                heads, whole = pl.ds(first, count), sources[index].shape[2] == local_rows
                source = sources[index].at[owner, heads] if whole else sources[index].at[owner, heads, rows]
                target = stage.at[owner, pl.ds(slab, count)]
                inward.append(pltpu.make_async_copy(source, target, arrivals.at[owner, part]))
                slab += count
        outward = []
        for index in range(owners // group):
            some = pl.ds(index * group, group)
            outward.append(pltpu.make_async_copy(stage.at[some], out.at[some], departures.at[index]))
        for copy in inward:
            copy.start()
        for index, departure in enumerate(outward):
            for copy in inward[index * group * len(plan) : (index + 1) * group * len(plan)]:
                copy.wait()
            departure.start()
        for departure in outward:
            departure.wait()

    shape = (owners, slabs, local_rows, width)
    return pl.pallas_call(
        kernel,
        grid_spec=pltpu.PrefetchScalarGridSpec(
            num_scalar_prefetch=1,
            grid=(1,),
            in_specs=[pl.BlockSpec(memory_space=pltpu.HBM)] * len(arrays),
            out_specs=pl.BlockSpec(memory_space=pltpu.HBM),
            scratch_shapes=[
                pltpu.VMEM(shape, jnp.bfloat16),
                pltpu.SemaphoreType.DMA((owners, len(plan))),
                pltpu.SemaphoreType.DMA((owners // group,)),
            ],
        ),
        out_shape=pltpu.HBM(shape, jnp.bfloat16),
        compiler_params=pltpu.CompilerParams(vmem_limit_bytes=48 * 1024 * 1024),
        cost_estimate=pl.CostEstimate(flops=0, bytes_accessed=4 * math.prod(shape), transcendentals=0),
    )(place, *[in_hbm(array) for array in arrays])


def pack_each(place, arrays, steps, first, count):
    _, _, local_rows, width = arrays[0].shape
    heads = pl.ds(first, count)
    parts = len(arrays)

    def kernel(place, *refs):
        sources, outs, (stage, arrivals, departures) = refs[:parts], refs[parts:-3], refs[-3:]
        rows = pl.ds(place[0] * local_rows, local_rows)
        inward, outward = [], []
        for index, step in enumerate(steps):
            owner = place[1 + step]
            for part, source in enumerate(sources):
                piece = source.at[owner, heads] if source.shape[2] == local_rows else source.at[owner, heads, rows]
                inward.append(pltpu.make_async_copy(piece, stage.at[index, :, part], arrivals.at[index, part]))
            outward.append(pltpu.make_async_copy(stage.at[index], outs[index].at[0], departures.at[index]))
        for copy in inward:
            copy.start()
        for index, departure in enumerate(outward):
            for copy in inward[index * parts : (index + 1) * parts]:
                copy.wait()
            departure.start()
        for departure in outward:
            departure.wait()

    shape = (count, parts, local_rows, width)
    return pl.pallas_call(
        kernel,
        grid_spec=pltpu.PrefetchScalarGridSpec(
            num_scalar_prefetch=1,
            grid=(1,),
            in_specs=[pl.BlockSpec(memory_space=pltpu.HBM)] * parts,
            out_specs=[pl.BlockSpec(memory_space=pltpu.HBM)] * len(steps),
            scratch_shapes=[
                pltpu.VMEM((len(steps),) + shape, jnp.bfloat16),
                pltpu.SemaphoreType.DMA((len(steps), parts)),
                pltpu.SemaphoreType.DMA((len(steps),)),
            ],
        ),
        out_shape=[pltpu.HBM((1,) + shape, jnp.bfloat16)] * len(steps),
        compiler_params=pltpu.CompilerParams(vmem_limit_bytes=48 * 1024 * 1024),
        cost_estimate=pl.CostEstimate(flops=0, bytes_accessed=4 * len(steps) * math.prod(shape), transcendentals=0),
    )(place, *[in_hbm(array) for array in arrays])


def collect(place, early, late):
    owners, first, local_rows, width = early.shape
    count = late[0].shape[1]

    def kernel(place, early, *refs):
        late, (out, semaphores) = refs[:owners], refs[owners:]
        copies = []
        for index in range(owners):
            target = out.at[index, pl.ds(0, first)]
            copies.append(pltpu.make_async_copy(early.at[index], target, semaphores.at[0, index]))
            target = out.at[place[1 + index], pl.ds(first, count)]
            copies.append(pltpu.make_async_copy(late[index].at[0], target, semaphores.at[1, index]))
        for copy in copies:
            copy.start()
        for copy in copies:
            copy.wait()

    shape = (owners, first + count, local_rows, width)
    arrays = [pltpu.with_memory_space_constraint(array, pltpu.VMEM) for array in [early, *late]]
    return pl.pallas_call(
        kernel,
        grid_spec=pltpu.PrefetchScalarGridSpec(
            num_scalar_prefetch=1,
            grid=(1,),
            in_specs=[pl.BlockSpec(memory_space=pl.ANY)] * len(arrays),
            out_specs=pl.BlockSpec(memory_space=pltpu.HBM),
            scratch_shapes=[pltpu.SemaphoreType.DMA((2, owners))],
        ),
        out_shape=pltpu.HBM(shape, jnp.bfloat16),
        compiler_params=pltpu.CompilerParams(vmem_limit_bytes=16 * 1024 * 1024),
        cost_estimate=pl.CostEstimate(flops=0, bytes_accessed=4 * math.prod(shape), transcendentals=0),
    )(place, *arrays)


def after(value, *earlier):
    return lax.optimization_barrier((value, *earlier))[0]


def per_device(queries, stretch_keys, stretch_values, cache_keys, cache_values, rand_blocks):
    heads, local_rows, width = queries.shape
    side = lax.axis_index("cache")
    assert local_rows == BLK and lax.axis_size("cache") == 2
    place = jnp.reshape(side, (1,)).astype(jnp.int32)

    def to_sibling(value):
        return lax.ppermute(value, "cache", [(0, 1), (1, 0)])

    by_heads = heads % (2 * lax.axis_size("seq")) == 0
    axes = ("seq", "cache") if by_heads else "seq"
    owners = lax.axis_size(axes)
    owned = heads // owners
    arrays = [rows.reshape(owners, owned, rows.shape[1], width) for rows in (queries, stretch_keys, stretch_values)]
    caches = (cache_keys, to_sibling(cache_keys), cache_values, to_sibling(cache_values))

    def exchange(value):
        return lax.all_to_all(value, axes, split_axis=0, concat_axis=0, tiled=True)

    if owners != 16 or owned != OWNED:
        mine = exchange(pack(place, arrays, [(index, 0, owned) for index in range(3)]))
        theirs = None if by_heads else to_sibling(mine)
        attended = attend(place, rand_blocks, mine, theirs, caches, owned)
        return exchange(attended).reshape(heads, local_rows, width)

    here = 2 * lax.axis_index("seq") + side
    owner_at = jnp.stack([side] + [here ^ step ^ (8 * side) for step in range(owners)]).astype(jnp.int32)
    source_at = jnp.stack([side] + [here ^ step ^ (8 * (side ^ (step & 1))) for step in range(owners)]).astype(jnp.int32)
    sent, started = [], []

    def pairs_of(step):
        return [(index, index ^ step ^ (8 * (index & 1))) for index in range(owners)]

    def send(message, step):
        if len(sent) >= WINDOW:
            message = after(message, sent[-WINDOW], *started[-1:])
        started.append(message)
        sent.append(lax.ppermute(message, axes, pairs_of(step)))
        return sent[-1]

    early, late = [None] * owners, [None] * owners
    for step, message in zip(STEPS, pack_each(owner_at, arrays, STEPS, 0, EARLY)):
        early[step] = send(message, step)
    messages = pack_each(owner_at, arrays, STEPS, EARLY, owned - EARLY)
    both = jnp.concatenate([source_at, owner_at[1:]])
    attended = attend_pieces(both, rand_blocks, early, caches, owned, 0)[0]
    for index, (step, message) in enumerate(zip(STEPS, messages)):
        late[step] = send(message if index < GATE else after(message, attended), step)
    attended = after(attended, *late)
    taken = exchange(attended)
    parts = attend_pieces(both, rand_blocks, late, caches, owned, EARLY, True)
    returned = [None] * owners
    for step in STEPS:
        returned[step] = lax.ppermute(parts[step], axes, pairs_of(step))
    return collect(source_at, taken, returned).reshape(heads, local_rows, width)


def solution(mesh):
    placed = (
        P("groups", ("seq", "cache"), None),
        P("groups", "seq", None),
        P("groups", "seq", None),
        P(("groups", "seq"), "cache", None),
        P(("groups", "seq"), "cache", None),
        P("groups", None),
    )
    return jax.shard_map(
        per_device,
        mesh=mesh,
        in_specs=placed,
        out_specs=P("groups", ("seq", "cache"), None),
        check_vma=False,
    )
```

```python
import math

import jax
import jax.numpy as jnp
from jax import lax
from jax.experimental import pallas as pl
from jax.experimental.pallas import tpu as pltpu
from jax.sharding import PartitionSpec as P

BLK = 128
LISTED = 8
UNROLL = 16
OWNED = 4
EARLY = 2
WINDOW = 7
GATE = 6
STEPS = (0, 8, 1, 9, 2, 10, 3, 11, 4, 12, 5, 13, 6, 14, 7, 15)


def unroll_of(sources):
    return UNROLL if sources % UNROLL == 0 else 1


def listed_blocks(rand, prefix, block):
    own = prefix + block
    return [own - 2, own - 1, own, 0, 1] + [rand[block, column] for column in range(3)]


def fill(blocks, side, cached_mine, cached_theirs, sources, put):
    cached = cached_mine.shape[1] // BLK
    for index in range(cached):
        rows = pl.ds(index * BLK, BLK)
        blocks[side * cached + index] = put(cached_mine[0, rows, :])
        blocks[(1 - side) * cached + index] = put(cached_theirs[0, rows, :])
    for block, ref, index in sources:
        blocks[2 * cached + block] = put(ref[index])


def turned(block):
    return block.T


def same(block):
    return block


def probabilities(query, keys, listed):
    factor = math.log2(math.e) / math.sqrt(query.shape[-1])
    key_slot = lax.broadcasted_iota(jnp.int32, (BLK, BLK), 0)
    query_slot = lax.broadcasted_iota(jnp.int32, (BLK, BLK), 1)
    chosen = jnp.concatenate([keys[key_block] for key_block in listed], axis=0)
    scores = lax.dot_general(chosen, query, (((1,), (1,)), ((), ())), preferred_element_type=jnp.float32)
    diagonal = jnp.where(key_slot > query_slot, -jnp.inf, scores[2 * BLK : 3 * BLK])
    scores = jnp.concatenate([scores[: 2 * BLK], diagonal, scores[3 * BLK :]], axis=0)
    weights = jnp.exp2((scores - jnp.max(scores, axis=0, keepdims=True)) * factor)
    inverse = 1.0 / jnp.sum(weights, axis=0, keepdims=True)
    return (weights * inverse).astype(jnp.bfloat16)


def weighted(probs, values, listed):
    chosen = jnp.concatenate([values[key_block] for key_block in listed], axis=1)
    return jnp.dot(chosen, probs, preferred_element_type=jnp.float32).T.astype(jnp.bfloat16)


def attention_kernel(paired, place, rand, queries, keys_mine, values_mine, ck_mine, ck_theirs, cv_mine, cv_theirs, *refs):
    theirs = refs[:2] if paired else None
    out, keys, values = refs[-3:]
    sources = queries.shape[0]
    prefix = 2 * ck_mine.shape[1] // BLK
    side = place[0]

    def block_of(source, which):
        return 2 * source + which if paired else source

    def rows_of(mine, part):
        rows = [(block_of(source, side), mine, (source, 0)) for source in range(sources)]
        if paired:
            rows += [(block_of(source, 1 - side), theirs[part], (source, 0)) for source in range(sources)]
        return rows

    fill(keys, side, ck_mine, ck_theirs, rows_of(keys_mine, 0), same)
    fill(values, side, cv_mine, cv_theirs, rows_of(values_mine, 1), turned)

    def one_block(source, carry):
        listed = listed_blocks(rand, prefix, block_of(source, side))
        out[source, 0] = weighted(probabilities(queries[source, 0], keys, listed), values, listed)
        return carry

    lax.fori_loop(0, sources, one_block, 0, unroll=unroll_of(sources))


def attend(place, rand, mine, theirs, caches, owned):
    sources, slabs, _, width = mine.shape
    heads = slabs // 3
    paired = theirs is not None
    cached_rows = caches[0].shape[1]
    key_blocks = 2 * cached_rows // BLK + (2 if paired else 1) * sources

    def slab(part):
        return pl.BlockSpec((sources, 1, BLK, width), lambda head, *_: (0, part * heads + head, 0, 0))

    def cache_index(head, place, rand):
        return ((0 if paired else place[0] * owned) + head, 0, 0)

    arrays = [in_hbm(array) for array in [mine] * 3 + list(caches) + ([theirs] * 2 if paired else [])]
    in_specs = [slab(0), slab(1), slab(2)] + [pl.BlockSpec((1, cached_rows, width), cache_index)] * 4
    in_specs += [slab(1), slab(2)] if paired else []
    work = heads * sources * BLK * LISTED * BLK
    return pl.pallas_call(
        lambda *refs: attention_kernel(paired, *refs),
        grid_spec=pltpu.PrefetchScalarGridSpec(
            num_scalar_prefetch=2,
            grid=(heads,),
            in_specs=in_specs,
            out_specs=pl.BlockSpec((sources, 1, BLK, width), lambda head, *_: (0, head, 0, 0)),
            scratch_shapes=[
                pltpu.VMEM((key_blocks, BLK, width), jnp.bfloat16),
                pltpu.VMEM((key_blocks, width, BLK), jnp.bfloat16),
            ],
        ),
        out_shape=jax.ShapeDtypeStruct((sources, owned, BLK, width), jnp.bfloat16),
        compiler_params=pltpu.CompilerParams(vmem_limit_bytes=48 * 1024 * 1024),
        cost_estimate=pl.CostEstimate(
            flops=4 * work * width,
            bytes_accessed=2 * heads * width * BLK * (4 * sources + 2 * key_blocks),
            transcendentals=work,
        ),
    )(place, rand, *arrays)


def pieces_kernel(pieces, by_step, place, rand, *refs):
    mine, (ck_mine, ck_theirs, cv_mine, cv_theirs) = refs[:pieces], refs[pieces : pieces + 4]
    keys, values, queries, results = refs[-4:]
    outs = refs[pieces + 4 : -4]
    prefix = 2 * ck_mine.shape[1] // BLK
    side = place[0]
    rows = [(place[1 + index], ref) for index, ref in enumerate(mine)]
    fill(keys, side, ck_mine, ck_theirs, [(source, ref, (0, 0, 1)) for source, ref in rows], same)
    fill(values, side, cv_mine, cv_theirs, [(source, ref, (0, 0, 2)) for source, ref in rows], turned)
    for source, ref in rows:
        queries[source] = ref[0, 0, 0]

    def one_block(source, carry):
        listed = listed_blocks(rand, prefix, source)
        results[source] = weighted(probabilities(queries[source], keys, listed), values, listed)
        return carry

    lax.fori_loop(0, pieces, one_block, 0, unroll=unroll_of(pieces))
    if by_step:
        for index, out in enumerate(outs):
            out[0, 0] = results[place[1 + pieces + index]]
    else:
        outs[0][:, 0] = results[...]


def attend_pieces(place, rand, mine, caches, owned, first, by_step=False):
    pieces = len(mine)
    _, heads, _, _, width = mine[0].shape
    cached_rows = caches[0].shape[1]
    key_blocks = 2 * cached_rows // BLK + pieces
    piece_spec = pl.BlockSpec((1, 1, 3, BLK, width), lambda head, *_: (0, head, 0, 0, 0))
    cache_spec = pl.BlockSpec((1, cached_rows, width), lambda head, place, rand: (place[0] * owned + first + head, 0, 0))
    arrays = [in_hbm(array) for array in [*mine, *caches]]
    in_specs = [piece_spec] * pieces + [cache_spec] * 4
    outs = pieces if by_step else 1
    work = heads * pieces * BLK * LISTED * BLK
    return pl.pallas_call(
        lambda *refs: pieces_kernel(pieces, by_step, *refs),
        grid_spec=pltpu.PrefetchScalarGridSpec(
            num_scalar_prefetch=2,
            grid=(heads,),
            in_specs=in_specs,
            out_specs=[pl.BlockSpec((pieces // outs, 1, BLK, width), lambda head, *_: (0, head, 0, 0))] * outs,
            scratch_shapes=[
                pltpu.VMEM((key_blocks, BLK, width), jnp.bfloat16),
                pltpu.VMEM((key_blocks, width, BLK), jnp.bfloat16),
                pltpu.VMEM((pieces, BLK, width), jnp.bfloat16),
                pltpu.VMEM((pieces, BLK, width), jnp.bfloat16),
            ],
        ),
        out_shape=[jax.ShapeDtypeStruct((pieces // outs, heads, BLK, width), jnp.bfloat16)] * outs,
        compiler_params=pltpu.CompilerParams(vmem_limit_bytes=48 * 1024 * 1024),
        cost_estimate=pl.CostEstimate(
            flops=24 * work * width,
            bytes_accessed=2 * heads * width * BLK * (4 * pieces + 2 * key_blocks),
            transcendentals=work,
        ),
    )(place, rand, *arrays)


def in_hbm(array):
    return pltpu.with_memory_space_constraint(array, pltpu.HBM)


def pack(place, arrays, plan):
    owners, _, local_rows, width = arrays[0].shape
    slabs = sum(count for _, _, count in plan)
    group = 4 if owners % 4 == 0 else 1

    def kernel(place, *refs):
        sources, (out, stage, arrivals, departures) = refs[:-4], refs[-4:]
        rows = pl.ds(place[0] * local_rows, local_rows)
        inward = []
        for owner in range(owners):
            slab = 0
            for part, (index, first, count) in enumerate(plan):
                heads, whole = pl.ds(first, count), sources[index].shape[2] == local_rows
                source = sources[index].at[owner, heads] if whole else sources[index].at[owner, heads, rows]
                target = stage.at[owner, pl.ds(slab, count)]
                inward.append(pltpu.make_async_copy(source, target, arrivals.at[owner, part]))
                slab += count
        outward = []
        for index in range(owners // group):
            some = pl.ds(index * group, group)
            outward.append(pltpu.make_async_copy(stage.at[some], out.at[some], departures.at[index]))
        for copy in inward:
            copy.start()
        for index, departure in enumerate(outward):
            for copy in inward[index * group * len(plan) : (index + 1) * group * len(plan)]:
                copy.wait()
            departure.start()
        for departure in outward:
            departure.wait()

    shape = (owners, slabs, local_rows, width)
    return pl.pallas_call(
        kernel,
        grid_spec=pltpu.PrefetchScalarGridSpec(
            num_scalar_prefetch=1,
            grid=(1,),
            in_specs=[pl.BlockSpec(memory_space=pltpu.HBM)] * len(arrays),
            out_specs=pl.BlockSpec(memory_space=pltpu.HBM),
            scratch_shapes=[
                pltpu.VMEM(shape, jnp.bfloat16),
                pltpu.SemaphoreType.DMA((owners, len(plan))),
                pltpu.SemaphoreType.DMA((owners // group,)),
            ],
        ),
        out_shape=pltpu.HBM(shape, jnp.bfloat16),
        compiler_params=pltpu.CompilerParams(vmem_limit_bytes=48 * 1024 * 1024),
        cost_estimate=pl.CostEstimate(flops=0, bytes_accessed=4 * math.prod(shape), transcendentals=0),
    )(place, *[in_hbm(array) for array in arrays])


def pack_each(place, arrays, steps, first, count):
    _, _, local_rows, width = arrays[0].shape
    heads = pl.ds(first, count)
    parts = len(arrays)

    def kernel(place, *refs):
        sources, outs, (stage, arrivals, departures) = refs[:parts], refs[parts:-3], refs[-3:]
        rows = pl.ds(place[0] * local_rows, local_rows)
        inward, outward = [], []
        for index, step in enumerate(steps):
            owner = place[1 + step]
            for part, source in enumerate(sources):
                piece = source.at[owner, heads] if source.shape[2] == local_rows else source.at[owner, heads, rows]
                inward.append(pltpu.make_async_copy(piece, stage.at[index, :, part], arrivals.at[index, part]))
            outward.append(pltpu.make_async_copy(stage.at[index], outs[index].at[0], departures.at[index]))
        for copy in inward:
            copy.start()
        for index, departure in enumerate(outward):
            for copy in inward[index * parts : (index + 1) * parts]:
                copy.wait()
            departure.start()
        for departure in outward:
            departure.wait()

    shape = (count, parts, local_rows, width)
    return pl.pallas_call(
        kernel,
        grid_spec=pltpu.PrefetchScalarGridSpec(
            num_scalar_prefetch=1,
            grid=(1,),
            in_specs=[pl.BlockSpec(memory_space=pltpu.HBM)] * parts,
            out_specs=[pl.BlockSpec(memory_space=pltpu.HBM)] * len(steps),
            scratch_shapes=[
                pltpu.VMEM((len(steps),) + shape, jnp.bfloat16),
                pltpu.SemaphoreType.DMA((len(steps), parts)),
                pltpu.SemaphoreType.DMA((len(steps),)),
            ],
        ),
        out_shape=[pltpu.HBM((1,) + shape, jnp.bfloat16)] * len(steps),
        compiler_params=pltpu.CompilerParams(vmem_limit_bytes=48 * 1024 * 1024),
        cost_estimate=pl.CostEstimate(flops=0, bytes_accessed=4 * len(steps) * math.prod(shape), transcendentals=0),
    )(place, *[in_hbm(array) for array in arrays])


def collect(place, early, late):
    owners, first, local_rows, width = early.shape
    count = late[0].shape[1]

    def kernel(place, early, *refs):
        late, (out, semaphores) = refs[:owners], refs[owners:]
        copies = []
        for index in range(owners):
            target = out.at[index, pl.ds(0, first)]
            copies.append(pltpu.make_async_copy(early.at[index], target, semaphores.at[0, index]))
            target = out.at[place[1 + index], pl.ds(first, count)]
            copies.append(pltpu.make_async_copy(late[index].at[0], target, semaphores.at[1, index]))
        for copy in copies:
            copy.start()
        for copy in copies:
            copy.wait()

    shape = (owners, first + count, local_rows, width)
    arrays = [pltpu.with_memory_space_constraint(array, pltpu.VMEM) for array in [early, *late]]
    return pl.pallas_call(
        kernel,
        grid_spec=pltpu.PrefetchScalarGridSpec(
            num_scalar_prefetch=1,
            grid=(1,),
            in_specs=[pl.BlockSpec(memory_space=pl.ANY)] * len(arrays),
            out_specs=pl.BlockSpec(memory_space=pltpu.HBM),
            scratch_shapes=[pltpu.SemaphoreType.DMA((2, owners))],
        ),
        out_shape=pltpu.HBM(shape, jnp.bfloat16),
        compiler_params=pltpu.CompilerParams(vmem_limit_bytes=16 * 1024 * 1024),
        cost_estimate=pl.CostEstimate(flops=0, bytes_accessed=4 * math.prod(shape), transcendentals=0),
    )(place, *arrays)


def after(value, *earlier):
    return lax.optimization_barrier((value, *earlier))[0]


def per_device(queries, stretch_keys, stretch_values, cache_keys, cache_values, rand_blocks):
    heads, local_rows, width = queries.shape
    side = lax.axis_index("cache")
    assert local_rows == BLK and lax.axis_size("cache") == 2
    place = jnp.reshape(side, (1,)).astype(jnp.int32)

    def to_sibling(value):
        return lax.ppermute(value, "cache", [(0, 1), (1, 0)])

    by_heads = heads % (2 * lax.axis_size("seq")) == 0
    axes = ("seq", "cache") if by_heads else "seq"
    owners = lax.axis_size(axes)
    owned = heads // owners
    arrays = [rows.reshape(owners, owned, rows.shape[1], width) for rows in (queries, stretch_keys, stretch_values)]
    caches = (cache_keys, to_sibling(cache_keys), cache_values, to_sibling(cache_values))

    def exchange(value):
        return lax.all_to_all(value, axes, split_axis=0, concat_axis=0, tiled=True)

    if owners != 16 or owned != OWNED:
        mine = exchange(pack(place, arrays, [(index, 0, owned) for index in range(3)]))
        theirs = None if by_heads else to_sibling(mine)
        attended = attend(place, rand_blocks, mine, theirs, caches, owned)
        return exchange(attended).reshape(heads, local_rows, width)

    here = 2 * lax.axis_index("seq") + side
    owner_at = jnp.stack([side] + [here ^ step ^ (8 * side) for step in range(owners)]).astype(jnp.int32)
    source_at = jnp.stack([side] + [here ^ step ^ (8 * (side ^ (step & 1))) for step in range(owners)]).astype(jnp.int32)
    sent, started = [], []

    def pairs_of(step):
        return [(index, index ^ step ^ (8 * (index & 1))) for index in range(owners)]

    def send(message, step):
        if len(sent) >= WINDOW:
            message = after(message, sent[-WINDOW], *started[-1:])
        started.append(message)
        sent.append(lax.ppermute(message, axes, pairs_of(step)))
        return sent[-1]

    early, late = [None] * owners, [None] * owners
    for step, message in zip(STEPS, pack_each(owner_at, arrays, STEPS, 0, EARLY)):
        early[step] = send(message, step)
    messages = pack_each(owner_at, arrays, STEPS, EARLY, owned - EARLY)
    both = jnp.concatenate([source_at, owner_at[1:]])
    attended = attend_pieces(both, rand_blocks, early, caches, owned, 0)[0]
    for index, (step, message) in enumerate(zip(STEPS, messages)):
        late[step] = send(message if index < GATE else after(message, attended), step)
    attended = after(attended, *late)
    taken = exchange(attended)
    parts = attend_pieces(both, rand_blocks, late, caches, owned, EARLY, True)
    returned = [None] * owners
    for step in STEPS:
        returned[step] = lax.ppermute(parts[step], axes, pairs_of(step))
    return collect(source_at, taken, returned).reshape(heads, local_rows, width)


def solution(mesh):
    placed = (
        P("groups", ("seq", "cache"), None),
        P("groups", "seq", None),
        P("groups", "seq", None),
        P(("groups", "seq"), "cache", None),
        P(("groups", "seq"), "cache", None),
        P("groups", None),
    )
    return jax.shard_map(
        per_device,
        mesh=mesh,
        in_specs=placed,
        out_specs=P("groups", ("seq", "cache"), None),
        check_vma=False,
    )
```

```python
import math

import jax
import jax.numpy as jnp
from jax import lax
from jax.experimental import pallas as pl
from jax.experimental.pallas import tpu as pltpu
from jax.sharding import PartitionSpec as P

BLK = 128
LISTED = 8
UNROLL = 16
OWNED = 4
EARLY = 2
WINDOW = 8
GATE = 7
STEPS = (0, 8, 1, 9, 2, 10, 3, 11, 4, 12, 5, 13, 6, 14, 7, 15)


def unroll_of(sources):
    return UNROLL if sources % UNROLL == 0 else 1


def listed_blocks(rand, prefix, block):
    own = prefix + block
    return [own - 2, own - 1, own, 0, 1] + [rand[block, column] for column in range(3)]


def fill(blocks, side, cached_mine, cached_theirs, sources, put):
    cached = cached_mine.shape[1] // BLK
    for index in range(cached):
        rows = pl.ds(index * BLK, BLK)
        blocks[side * cached + index] = put(cached_mine[0, rows, :])
        blocks[(1 - side) * cached + index] = put(cached_theirs[0, rows, :])
    for block, ref, index in sources:
        blocks[2 * cached + block] = put(ref[index])


def turned(block):
    return block.T


def same(block):
    return block


def probabilities(query, keys, listed):
    factor = math.log2(math.e) / math.sqrt(query.shape[-1])
    key_slot = lax.broadcasted_iota(jnp.int32, (BLK, BLK), 0)
    query_slot = lax.broadcasted_iota(jnp.int32, (BLK, BLK), 1)
    chosen = jnp.concatenate([keys[key_block] for key_block in listed], axis=0)
    scores = lax.dot_general(chosen, query, (((1,), (1,)), ((), ())), preferred_element_type=jnp.float32)
    diagonal = jnp.where(key_slot > query_slot, -jnp.inf, scores[2 * BLK : 3 * BLK])
    scores = jnp.concatenate([scores[: 2 * BLK], diagonal, scores[3 * BLK :]], axis=0)
    weights = jnp.exp2((scores - jnp.max(scores, axis=0, keepdims=True)) * factor)
    inverse = 1.0 / jnp.sum(weights, axis=0, keepdims=True)
    return (weights * inverse).astype(jnp.bfloat16)


def weighted(probs, values, listed):
    chosen = jnp.concatenate([values[key_block] for key_block in listed], axis=1)
    return jnp.dot(chosen, probs, preferred_element_type=jnp.float32).T.astype(jnp.bfloat16)


def attention_kernel(paired, place, rand, queries, keys_mine, values_mine, ck_mine, ck_theirs, cv_mine, cv_theirs, *refs):
    theirs = refs[:2] if paired else None
    out, keys, values = refs[-3:]
    sources = queries.shape[0]
    prefix = 2 * ck_mine.shape[1] // BLK
    side = place[0]

    def block_of(source, which):
        return 2 * source + which if paired else source

    def rows_of(mine, part):
        rows = [(block_of(source, side), mine, (source, 0)) for source in range(sources)]
        if paired:
            rows += [(block_of(source, 1 - side), theirs[part], (source, 0)) for source in range(sources)]
        return rows

    fill(keys, side, ck_mine, ck_theirs, rows_of(keys_mine, 0), same)
    fill(values, side, cv_mine, cv_theirs, rows_of(values_mine, 1), turned)

    def one_block(source, carry):
        listed = listed_blocks(rand, prefix, block_of(source, side))
        out[source, 0] = weighted(probabilities(queries[source, 0], keys, listed), values, listed)
        return carry

    lax.fori_loop(0, sources, one_block, 0, unroll=unroll_of(sources))


def attend(place, rand, mine, theirs, caches, owned):
    sources, slabs, _, width = mine.shape
    heads = slabs // 3
    paired = theirs is not None
    cached_rows = caches[0].shape[1]
    key_blocks = 2 * cached_rows // BLK + (2 if paired else 1) * sources

    def slab(part):
        return pl.BlockSpec((sources, 1, BLK, width), lambda head, *_: (0, part * heads + head, 0, 0))

    def cache_index(head, place, rand):
        return ((0 if paired else place[0] * owned) + head, 0, 0)

    arrays = [in_hbm(array) for array in [mine] * 3 + list(caches) + ([theirs] * 2 if paired else [])]
    in_specs = [slab(0), slab(1), slab(2)] + [pl.BlockSpec((1, cached_rows, width), cache_index)] * 4
    in_specs += [slab(1), slab(2)] if paired else []
    work = heads * sources * BLK * LISTED * BLK
    return pl.pallas_call(
        lambda *refs: attention_kernel(paired, *refs),
        grid_spec=pltpu.PrefetchScalarGridSpec(
            num_scalar_prefetch=2,
            grid=(heads,),
            in_specs=in_specs,
            out_specs=pl.BlockSpec((sources, 1, BLK, width), lambda head, *_: (0, head, 0, 0)),
            scratch_shapes=[
                pltpu.VMEM((key_blocks, BLK, width), jnp.bfloat16),
                pltpu.VMEM((key_blocks, width, BLK), jnp.bfloat16),
            ],
        ),
        out_shape=jax.ShapeDtypeStruct((sources, owned, BLK, width), jnp.bfloat16),
        compiler_params=pltpu.CompilerParams(vmem_limit_bytes=48 * 1024 * 1024),
        cost_estimate=pl.CostEstimate(
            flops=4 * work * width,
            bytes_accessed=2 * heads * width * BLK * (4 * sources + 2 * key_blocks),
            transcendentals=work,
        ),
    )(place, rand, *arrays)


def pieces_kernel(pieces, by_step, place, rand, *refs):
    mine, (ck_mine, ck_theirs, cv_mine, cv_theirs) = refs[:pieces], refs[pieces : pieces + 4]
    keys, values, queries, results = refs[-4:]
    outs = refs[pieces + 4 : -4]
    prefix = 2 * ck_mine.shape[1] // BLK
    side = place[0]
    rows = [(place[1 + index], ref) for index, ref in enumerate(mine)]
    fill(keys, side, ck_mine, ck_theirs, [(source, ref, (0, 0, 1)) for source, ref in rows], same)
    fill(values, side, cv_mine, cv_theirs, [(source, ref, (0, 0, 2)) for source, ref in rows], turned)
    for source, ref in rows:
        queries[source] = ref[0, 0, 0]

    def one_block(source, carry):
        listed = listed_blocks(rand, prefix, source)
        results[source] = weighted(probabilities(queries[source], keys, listed), values, listed)
        return carry

    lax.fori_loop(0, pieces, one_block, 0, unroll=unroll_of(pieces))
    if by_step:
        for index, out in enumerate(outs):
            out[0, 0] = results[place[1 + pieces + index]]
    else:
        outs[0][:, 0] = results[...]


def attend_pieces(place, rand, mine, caches, owned, first, by_step=False):
    pieces = len(mine)
    _, heads, _, _, width = mine[0].shape
    cached_rows = caches[0].shape[1]
    key_blocks = 2 * cached_rows // BLK + pieces
    piece_spec = pl.BlockSpec((1, 1, 3, BLK, width), lambda head, *_: (0, head, 0, 0, 0))
    cache_spec = pl.BlockSpec((1, cached_rows, width), lambda head, place, rand: (place[0] * owned + first + head, 0, 0))
    arrays = [in_hbm(array) for array in [*mine, *caches]]
    in_specs = [piece_spec] * pieces + [cache_spec] * 4
    outs = pieces if by_step else 1
    work = heads * pieces * BLK * LISTED * BLK
    return pl.pallas_call(
        lambda *refs: pieces_kernel(pieces, by_step, *refs),
        grid_spec=pltpu.PrefetchScalarGridSpec(
            num_scalar_prefetch=2,
            grid=(heads,),
            in_specs=in_specs,
            out_specs=[pl.BlockSpec((pieces // outs, 1, BLK, width), lambda head, *_: (0, head, 0, 0))] * outs,
            scratch_shapes=[
                pltpu.VMEM((key_blocks, BLK, width), jnp.bfloat16),
                pltpu.VMEM((key_blocks, width, BLK), jnp.bfloat16),
                pltpu.VMEM((pieces, BLK, width), jnp.bfloat16),
                pltpu.VMEM((pieces, BLK, width), jnp.bfloat16),
            ],
        ),
        out_shape=[jax.ShapeDtypeStruct((pieces // outs, heads, BLK, width), jnp.bfloat16)] * outs,
        compiler_params=pltpu.CompilerParams(vmem_limit_bytes=48 * 1024 * 1024),
        cost_estimate=pl.CostEstimate(
            flops=24 * work * width,
            bytes_accessed=2 * heads * width * BLK * (4 * pieces + 2 * key_blocks),
            transcendentals=work,
        ),
    )(place, rand, *arrays)


def in_hbm(array):
    return pltpu.with_memory_space_constraint(array, pltpu.HBM)


def pack(place, arrays, plan):
    owners, _, local_rows, width = arrays[0].shape
    slabs = sum(count for _, _, count in plan)
    group = 4 if owners % 4 == 0 else 1

    def kernel(place, *refs):
        sources, (out, stage, arrivals, departures) = refs[:-4], refs[-4:]
        rows = pl.ds(place[0] * local_rows, local_rows)
        inward = []
        for owner in range(owners):
            slab = 0
            for part, (index, first, count) in enumerate(plan):
                heads, whole = pl.ds(first, count), sources[index].shape[2] == local_rows
                source = sources[index].at[owner, heads] if whole else sources[index].at[owner, heads, rows]
                target = stage.at[owner, pl.ds(slab, count)]
                inward.append(pltpu.make_async_copy(source, target, arrivals.at[owner, part]))
                slab += count
        outward = []
        for index in range(owners // group):
            some = pl.ds(index * group, group)
            outward.append(pltpu.make_async_copy(stage.at[some], out.at[some], departures.at[index]))
        for copy in inward:
            copy.start()
        for index, departure in enumerate(outward):
            for copy in inward[index * group * len(plan) : (index + 1) * group * len(plan)]:
                copy.wait()
            departure.start()
        for departure in outward:
            departure.wait()

    shape = (owners, slabs, local_rows, width)
    return pl.pallas_call(
        kernel,
        grid_spec=pltpu.PrefetchScalarGridSpec(
            num_scalar_prefetch=1,
            grid=(1,),
            in_specs=[pl.BlockSpec(memory_space=pltpu.HBM)] * len(arrays),
            out_specs=pl.BlockSpec(memory_space=pltpu.HBM),
            scratch_shapes=[
                pltpu.VMEM(shape, jnp.bfloat16),
                pltpu.SemaphoreType.DMA((owners, len(plan))),
                pltpu.SemaphoreType.DMA((owners // group,)),
            ],
        ),
        out_shape=pltpu.HBM(shape, jnp.bfloat16),
        compiler_params=pltpu.CompilerParams(vmem_limit_bytes=48 * 1024 * 1024),
        cost_estimate=pl.CostEstimate(flops=0, bytes_accessed=4 * math.prod(shape), transcendentals=0),
    )(place, *[in_hbm(array) for array in arrays])


def pack_each(place, arrays, steps, first, count):
    _, _, local_rows, width = arrays[0].shape
    heads = pl.ds(first, count)
    parts = len(arrays)

    def kernel(place, *refs):
        sources, outs, (stage, arrivals, departures) = refs[:parts], refs[parts:-3], refs[-3:]
        rows = pl.ds(place[0] * local_rows, local_rows)
        inward, outward = [], []
        for index, step in enumerate(steps):
            owner = place[1 + step]
            for part, source in enumerate(sources):
                piece = source.at[owner, heads] if source.shape[2] == local_rows else source.at[owner, heads, rows]
                inward.append(pltpu.make_async_copy(piece, stage.at[index, :, part], arrivals.at[index, part]))
            outward.append(pltpu.make_async_copy(stage.at[index], outs[index].at[0], departures.at[index]))
        for copy in inward:
            copy.start()
        for index, departure in enumerate(outward):
            for copy in inward[index * parts : (index + 1) * parts]:
                copy.wait()
            departure.start()
        for departure in outward:
            departure.wait()

    shape = (count, parts, local_rows, width)
    return pl.pallas_call(
        kernel,
        grid_spec=pltpu.PrefetchScalarGridSpec(
            num_scalar_prefetch=1,
            grid=(1,),
            in_specs=[pl.BlockSpec(memory_space=pltpu.HBM)] * parts,
            out_specs=[pl.BlockSpec(memory_space=pltpu.HBM)] * len(steps),
            scratch_shapes=[
                pltpu.VMEM((len(steps),) + shape, jnp.bfloat16),
                pltpu.SemaphoreType.DMA((len(steps), parts)),
                pltpu.SemaphoreType.DMA((len(steps),)),
            ],
        ),
        out_shape=[pltpu.HBM((1,) + shape, jnp.bfloat16)] * len(steps),
        compiler_params=pltpu.CompilerParams(vmem_limit_bytes=48 * 1024 * 1024),
        cost_estimate=pl.CostEstimate(flops=0, bytes_accessed=4 * len(steps) * math.prod(shape), transcendentals=0),
    )(place, *[in_hbm(array) for array in arrays])


def collect(place, early, late):
    owners, first, local_rows, width = early.shape
    count = late[0].shape[1]

    def kernel(place, early, *refs):
        late, (out, semaphores) = refs[:owners], refs[owners:]
        copies = []
        for index in range(owners):
            target = out.at[index, pl.ds(0, first)]
            copies.append(pltpu.make_async_copy(early.at[index], target, semaphores.at[0, index]))
            target = out.at[place[1 + index], pl.ds(first, count)]
            copies.append(pltpu.make_async_copy(late[index].at[0], target, semaphores.at[1, index]))
        for copy in copies:
            copy.start()
        for copy in copies:
            copy.wait()

    shape = (owners, first + count, local_rows, width)
    arrays = [pltpu.with_memory_space_constraint(array, pltpu.VMEM) for array in [early, *late]]
    return pl.pallas_call(
        kernel,
        grid_spec=pltpu.PrefetchScalarGridSpec(
            num_scalar_prefetch=1,
            grid=(1,),
            in_specs=[pl.BlockSpec(memory_space=pl.ANY)] * len(arrays),
            out_specs=pl.BlockSpec(memory_space=pltpu.HBM),
            scratch_shapes=[pltpu.SemaphoreType.DMA((2, owners))],
        ),
        out_shape=pltpu.HBM(shape, jnp.bfloat16),
        compiler_params=pltpu.CompilerParams(vmem_limit_bytes=16 * 1024 * 1024),
        cost_estimate=pl.CostEstimate(flops=0, bytes_accessed=4 * math.prod(shape), transcendentals=0),
    )(place, *arrays)


def after(value, *earlier):
    return lax.optimization_barrier((value, *earlier))[0]


def per_device(queries, stretch_keys, stretch_values, cache_keys, cache_values, rand_blocks):
    heads, local_rows, width = queries.shape
    side = lax.axis_index("cache")
    assert local_rows == BLK and lax.axis_size("cache") == 2
    place = jnp.reshape(side, (1,)).astype(jnp.int32)

    def to_sibling(value):
        return lax.ppermute(value, "cache", [(0, 1), (1, 0)])

    by_heads = heads % (2 * lax.axis_size("seq")) == 0
    axes = ("seq", "cache") if by_heads else "seq"
    owners = lax.axis_size(axes)
    owned = heads // owners
    arrays = [rows.reshape(owners, owned, rows.shape[1], width) for rows in (queries, stretch_keys, stretch_values)]
    caches = (cache_keys, to_sibling(cache_keys), cache_values, to_sibling(cache_values))

    def exchange(value):
        return lax.all_to_all(value, axes, split_axis=0, concat_axis=0, tiled=True)

    if owners != 16 or owned != OWNED:
        mine = exchange(pack(place, arrays, [(index, 0, owned) for index in range(3)]))
        theirs = None if by_heads else to_sibling(mine)
        attended = attend(place, rand_blocks, mine, theirs, caches, owned)
        return exchange(attended).reshape(heads, local_rows, width)

    here = 2 * lax.axis_index("seq") + side
    owner_at = jnp.stack([side] + [here ^ step ^ (8 * side) for step in range(owners)]).astype(jnp.int32)
    source_at = jnp.stack([side] + [here ^ step ^ (8 * (side ^ (step & 1))) for step in range(owners)]).astype(jnp.int32)
    sent, started = [], []

    def pairs_of(step):
        return [(index, index ^ step ^ (8 * (index & 1))) for index in range(owners)]

    def send(message, step):
        if len(sent) >= WINDOW:
            message = after(message, sent[-WINDOW], *started[-1:])
        started.append(message)
        sent.append(lax.ppermute(message, axes, pairs_of(step)))
        return sent[-1]

    early, late = [None] * owners, [None] * owners
    for step, message in zip(STEPS, pack_each(owner_at, arrays, STEPS, 0, EARLY)):
        early[step] = send(message, step)
    messages = pack_each(owner_at, arrays, STEPS, EARLY, owned - EARLY)
    both = jnp.concatenate([source_at, owner_at[1:]])
    attended = attend_pieces(both, rand_blocks, early, caches, owned, 0)[0]
    for index, (step, message) in enumerate(zip(STEPS, messages)):
        late[step] = send(message if index < GATE else after(message, attended), step)
    attended = after(attended, *late)
    taken = exchange(attended)
    parts = attend_pieces(both, rand_blocks, late, caches, owned, EARLY, True)
    returned = [None] * owners
    for step in STEPS:
        returned[step] = lax.ppermute(parts[step], axes, pairs_of(step))
    return collect(source_at, taken, returned).reshape(heads, local_rows, width)


def solution(mesh):
    placed = (
        P("groups", ("seq", "cache"), None),
        P("groups", "seq", None),
        P("groups", "seq", None),
        P(("groups", "seq"), "cache", None),
        P(("groups", "seq"), "cache", None),
        P("groups", None),
    )
    return jax.shard_map(
        per_device,
        mesh=mesh,
        in_specs=placed,
        out_specs=P("groups", ("seq", "cache"), None),
        check_vma=False,
    )
```
